32 devices in a mesh: dp: 4 (over z), gx: 2 (over x), gy: 4 (over y, core).
Axes of the slice: x: 2, y: 2, z: 4, core: 2. Of those that a mesh axis runs over, the one named last changes fastest.
Arguments:
- volume: bfloat16 [4, 8, 64, 8, 128], P('dp', 'gx', 'gy'), may hold values from -6 to 6
- cotangent: bfloat16 [4, 8, 64, 8, 128], P('dp', 'gx', 'gy'), may hold values from -1 to 1
- master: float32 [6912, 128], P('dp'), may hold values from -0.109375 to 0.109375
- moment_one: float32 [6912, 128], P('dp'), may hold values from -6 to 6
- moment_two: float32 [6912, 128], P('dp'), may hold values from 0.25 to 4
Outputs:
- activation: bfloat16 [4, 8, 64, 8, 128], P('dp', 'gx', 'gy')
- new_master: float32 [6912, 128], P('dp')
- new_moment_one: float32 [6912, 128], P('dp')
- new_moment_two: float32 [6912, 128], P('dp')
The draws below stay inside these ranges and needn't reach their ends.
All inputs are finite; a program needn't handle non-finite values.
Results may differ from the reference program's by a relative error of at most 0.006.
The reference program's roundings to bfloat16 on the way (of `kernels`, `hidden`, `delta_two` and `delta_one`) count: a program that leaves them out, or rounds other values in their place, can miss the bound.
Values may be sent and summed in bfloat16 or wider, within the bound.
A program may use at most 64 MiB of HBM per device.

```python
import math
import jax
import jax.numpy as jnp
from jax import lax

C = 128
CZ = 8
VOLUMES = 4
NX = 8
NY = 64
PROWS = 6912


def shard_levels(stream_key, extent, cuts, low, high):
    gain, own = 1.0, jax.random.fold_in(stream_key, 6)
    for position, parts in cuts:
        draws = jnp.exp(jax.random.uniform(jax.random.fold_in(own, position), (parts,), jnp.float32, low / len(cuts), high / len(cuts)))
        gain = gain * jnp.repeat(draws, extent[position] // parts).reshape([-1 if axis == position else 1 for axis in range(len(extent))])
    return gain


def normal_values(key, shape, deviation, reach, split=(), held_as=jnp.bfloat16):
    loudness = shard_levels(key, shape, split, -0.22, 0.18) if split else 1.0
    entries = jax.random.normal(key, shape, jnp.float32) * deviation * loudness
    return jnp.minimum(jnp.maximum(entries, -reach), reach).astype(held_as)


def setup_inputs(seed: int = 0) -> dict:
    splits = jax.random.split(jax.random.key(seed), 6)
    volume = normal_values(splits[0], (VOLUMES, NX, NY, CZ, C), 1.0, 6.0, ((0, 4), (1, 2), (2, 4)))
    cotangent = normal_values(splits[1], (VOLUMES, NX, NY, CZ, C), (8.0 / (VOLUMES * NX * NY * CZ) ** 0.5), 1.0, ((0, 4), (1, 2), (2, 4)))
    master = normal_values(splits[2], (PROWS, C), (27 * C) ** -0.5, 0.109375, ((0, 4),), jnp.float32)
    moment_one = normal_values(splits[3], (PROWS, C), 1.0, 6.0, ((0, 4),), jnp.float32)
    moment_two = jnp.clip(jnp.exp(math.log(4.0) - 2.7725887 * jax.random.uniform(splits[4], (PROWS, C), jnp.float32) ** shard_levels(splits[4], (PROWS, C), ((0, 4),), -0.2, 0.2)), 0.25, 4.0)
    return dict(volume=volume, cotangent=cotangent, master=master, moment_one=moment_one, moment_two=moment_two)


inv_root_two = 0.7071067811865476
inv_root_tau = 0.3989422804014327
beta_one = 0.9
beta_two = 0.999
learn_rate = 0.01
epsilon = 1e-08

def gelu_value(field):
    return 0.5 * field * (1.0 + lax.erf(field * inv_root_two))

def gelu_slope(field):
    normal_cdf = 0.5 * (1.0 + lax.erf(field * inv_root_two))
    return normal_cdf + field * jnp.exp(-0.5 * field * field) * inv_root_tau

def pad_all(field):
    return jnp.pad(field, ((1, 1), (1, 1), (1, 1), (0, 0)))

def convolve(padded, kernel):
    span_x = padded.shape[0] - 2
    span_y = padded.shape[1] - 2
    span_z = padded.shape[2] - 2
    total = jnp.zeros((span_x * span_y * span_z, kernel.shape[2]), jnp.float32)
    for offset_x in range(3):
        for offset_y in range(3):
            for offset_z in range(3):
                window = padded[offset_x:offset_x + span_x, offset_y:offset_y + span_y, offset_z:offset_z + span_z]
                total = total + jnp.dot(window.reshape(-1, padded.shape[3]), kernel[9 * offset_x + 3 * offset_y + offset_z], preferred_element_type=jnp.float32)
    return total.reshape(span_x, span_y, span_z, kernel.shape[2])

def kernel_grad(padded, delta):
    flat_delta = delta.reshape(-1, delta.shape[3])
    span_x, span_y, span_z = (delta.shape[0], delta.shape[1], delta.shape[2])
    pieces = []
    for offset_x in range(3):
        for offset_y in range(3):
            for offset_z in range(3):
                window = padded[offset_x:offset_x + span_x, offset_y:offset_y + span_y, offset_z:offset_z + span_z]
                pieces.append(jnp.dot(window.reshape(-1, padded.shape[3]).T, flat_delta, preferred_element_type=jnp.float32))
    return jnp.stack(pieces)

def adam_update(master, moment_one, moment_two, gradient):
    new_one = beta_one * moment_one + (1.0 - beta_one) * gradient
    new_two = beta_two * moment_two + (1.0 - beta_two) * gradient * gradient
    update = new_one / (1.0 - beta_one ** 10) / (jnp.sqrt(new_two / (1.0 - beta_two ** 10)) + epsilon)
    return (master - learn_rate * update, new_one, new_two)

def reference(volume, cotangent, master, moment_one, moment_two):
    kernels = master.astype(jnp.bfloat16).reshape(2, 27, C, C)
    flipped = kernels[1][::-1].transpose(0, 2, 1)

    def single(pair):
        field, upstream = pair
        padded_in = pad_all(field)
        first = convolve(padded_in, kernels[0])
        hidden = gelu_value(first).astype(jnp.bfloat16)
        padded_hidden = pad_all(hidden)
        second = convolve(padded_hidden, kernels[1])
        result = gelu_value(second).astype(jnp.bfloat16)
        delta_two = (upstream.astype(jnp.float32) * gelu_slope(second)).astype(jnp.bfloat16)
        grad_two = kernel_grad(padded_hidden, delta_two)
        back = convolve(pad_all(delta_two), flipped)
        delta_one = (back * gelu_slope(first)).astype(jnp.bfloat16)
        grad_one = kernel_grad(padded_in, delta_one)
        return (result, jnp.stack([grad_one, grad_two]))
    results, grads = lax.map(single, (volume, cotangent))
    gradient = lax.optimization_barrier(jnp.sum(grads, axis=0)).reshape(54 * C, C)
    new_master, new_one, new_two = adam_update(master, moment_one, moment_two, gradient)
    return (results, new_master, new_one, new_two)
```

```python
import functools

import jax
import jax.numpy as jnp
from jax import lax
from jax.experimental import pallas as pl
from jax.experimental.pallas import tpu as pltpu
from jax.sharding import PartitionSpec as P

inv_root_two = 0.7071067811865476
inv_root_tau = 0.3989422804014327
beta_one = 0.9
beta_two = 0.999
learn_rate = 0.01
epsilon = 1e-08
C = 128
HX, HY, CY = 3, 4, 2
MESH = pl.DeviceIdType.MESH
VMEM = pltpu.VMEM
f32, bf16 = jnp.float32, jnp.bfloat16


def gelu_value(field):
    return 0.5 * field * (1.0 + lax.erf(field * inv_root_two))


def gelu_slope(field):
    normal_cdf = 0.5 * (1.0 + lax.erf(field * inv_root_two))
    return normal_cdf + field * jnp.exp(-0.5 * field * field) * inv_root_tau


def place():
    d, x, y = lax.axis_index("dp"), lax.axis_index("gx"), lax.axis_index("gy")
    return d, x, y, lax.rem(x, 2), lax.rem(lax.div(y, 2), 2), lax.rem(y, 2)


def flip(index, bit, step):
    return index + step - 2 * step * bit


def gather_kernel(counts, vol, cot, master, vext, cext, w, hsend, hrecv, wsend, wrecv):
    D, GX, GY = counts
    d, x, y, bx, by, bc = place()
    sx, ry = vol.shape[0], vol.shape[1]
    H = master.shape[0]
    Q = H // 4
    here = {"x": (d, flip(x, bx, 1), y), "y": (d, x, flip(y, by, 2)), "c": (d, x, flip(y, bc, 1))}

    vext[...] = jnp.zeros_like(vext)
    cext[...] = jnp.zeros_like(cext)
    around = [(i, j) for i in (-1, 0, 1) for j in (-1, 0, 1) if (i, j) != (0, 0)]

    def exists(i, j):
        ok = None
        for value, step, count in ((x, i, GX), (y, j, GY)):
            if step:
                now = (value + step >= 0) & (value + step < count)
                ok = now if ok is None else ok & now
        return ok

    barrier = pltpu.get_barrier_semaphore()
    total = jnp.int32(3)
    for key in ("x", "y", "c"):
        pl.semaphore_signal(barrier, inc=1, device_id=here[key], device_id_type=MESH)
    for i, j in around:
        ok = exists(i, j)

        @pl.when(ok)
        def _(i=i, j=j):
            pl.semaphore_signal(barrier, inc=1, device_id=(d, x + i, y + j), device_id_type=MESH)

        total = total + jnp.where(ok, 1, 0)
    for step in (-1, 1):
        ok = (d + step >= 0) & (d + step < D)

        @pl.when(ok)
        def _(step=step):
            pl.semaphore_signal(barrier, inc=1, device_id=(d + step, x, y), device_id_type=MESH)

        total = total + jnp.where(ok, 1, 0)

    vext[pl.ds(HX, sx), pl.ds(8 * HY, ry)] = vol[...]
    cext[pl.ds(1, sx), pl.ds(8 * CY, ry)] = cot[...]
    w[pl.ds(pl.multiple_of(d * H, 16), H)] = master[...].astype(bf16)
    pl.semaphore_wait(barrier, total)

    def rows(s, q):
        return w.at[pl.ds(pl.multiple_of(s * H + q * Q, 16), Q)]

    def move(ref, k, s, target):
        return pltpu.make_async_remote_copy(
            src_ref=ref, dst_ref=ref, send_sem=wsend.at[k, s], recv_sem=wrecv.at[k, s],
            device_id=target, device_id_type=MESH,
        )

    def bit(s):
        even = lax.rem(s, 2) == 0
        return even, jnp.where(even, bx, by)

    def quarter(s):
        return 2 * bit(s)[1] + bc

    def other(s):
        return 2 * (1 - bit(s)[1]) + bc

    def up(s):
        return move(rows(s, quarter(s)), 0, s, (d + 1, x, y))

    def down(s):
        return move(rows(s, quarter(s)), 1, s, (d - 1, x, y))

    def partner(s, q):
        even = lax.rem(s, 2) == 0
        target = (d, jnp.where(even, here["x"][1], x), jnp.where(even, y, here["y"][2]))
        return move(rows(s, q), 2, s, target)

    def sibling(s, q, k):
        return move(rows(s, q), k, s, here["c"])

    @pl.when(d < D - 1)
    def _():
        up(d).start()

    @pl.when(d > 0)
    def _():
        down(d).start()

    def halo(n, i, j):
        def part(step, halo_x, size):
            if step < 0:
                return 0, halo_x + size, halo_x
            if step > 0:
                return size - halo_x, 0, halo_x
            return 0, halo_x, size

        copies = []
        for k, (src, dst, hx, hy) in enumerate(((vol, vext, HX, HY), (cot, cext, 1, CY))):
            xs, xd, xn = part(i, hx, sx)
            ys, yd, yn = part(j, 8 * hy, ry)
            copies.append(
                pltpu.make_async_remote_copy(
                    src_ref=src.at[pl.ds(xs, xn), pl.ds(ys, yn)],
                    dst_ref=dst.at[pl.ds(xd, xn), pl.ds(yd, yn)],
                    send_sem=hsend.at[k, n], recv_sem=hrecv.at[k, n],
                    device_id=(d, x + i, y + j), device_id_type=MESH,
                )
            )
        return copies

    for n, (i, j) in enumerate(around):
        @pl.when(exists(i, j))
        def _(n=n, i=i, j=j):
            for copy in halo(n, i, j):
                copy.start()

    def spread(s):
        partner(s, quarter(s)).start()
        sibling(s, quarter(s), 3).start()

    def pass_on(s):
        partner(s, other(s)).wait_recv()
        sibling(s, other(s), 4).start()

    for t in range(1, D):
        @pl.when(d - t >= 0)
        def _(t=t):
            s = d - t
            up(s).wait_recv()

            @pl.when(d < D - 1)
            def _():
                up(s).start()

            spread(s)

        @pl.when(d + t < D)
        def _(t=t):
            s = d + t
            down(s).wait_recv()

            @pl.when(d > 0)
            def _():
                down(s).start()

            spread(s)

        if t > 1:
            @pl.when(d - t + 1 >= 0)
            def _(t=t):
                pass_on(d - t + 1)

            @pl.when(d + t - 1 < D)
            def _(t=t):
                pass_on(d + t - 1)

    @pl.when(d - D + 1 >= 0)
    def _():
        pass_on(d - D + 1)

    @pl.when(d + D - 1 < D)
    def _():
        pass_on(d + D - 1)

    for t in range(1, D):
        for sign in (-1, 1):
            s = d + sign * t

            @pl.when((s >= 0) & (s < D))
            def _(s=s):
                theirs = 2 * bit(s)[1] + 1 - bc
                sibling(s, theirs, 3).wait_recv()
                sibling(s, 2 * (1 - bit(s)[1]) + 1 - bc, 4).wait_recv()
                partner(s, quarter(s)).wait_send()
                sibling(s, quarter(s), 3).wait_send()
                sibling(s, other(s), 4).wait_send()

    for s in range(D):
        @pl.when((s <= d) & (d < D - 1))
        def _(s=s):
            up(jnp.int32(s)).wait_send()

        @pl.when((s >= d) & (d > 0))
        def _(s=s):
            down(jnp.int32(s)).wait_send()

    for n, (i, j) in enumerate(around):
        @pl.when(exists(i, j))
        def _(n=n, i=i, j=j):
            for copy in halo(n, i, j):
                copy.wait_send()
            for copy in halo(7 - n, -i, -j):
                copy.wait_recv()


def shifted(field):
    rows = field.shape[0]
    z = lax.rem(lax.broadcasted_iota(jnp.int32, field.shape, 0), 8)
    before = jnp.where(z == 0, 0.0, pltpu.roll(field, 1, 0))
    after = jnp.where(z == 7, 0.0, pltpu.roll(field, rows - 1, 0))
    return before, field, after


def unfold(field, first, rows, out):
    views = shifted(field)
    for b in range(3):
        for c in range(3):
            k = 3 * b + c
            out[:, k * C : (k + 1) * C] = views[c][first + 8 * b : first + 8 * b + rows].astype(bf16)


def compute_kernel(counts, vext, cext, w, act, grad, x1, x2, x3, first, kt, d1, d2):
    D, GX, GY = counts
    sx = vext.shape[0] - 2 * HX
    ry = vext.shape[1] - 16 * HY
    gx, gy = lax.axis_index("gx"), lax.axis_index("gy")
    n1, n2 = ry + 32, ry + 16
    L = 9 * C

    d1[...] = jnp.zeros_like(d1)
    d2[...] = jnp.zeros_like(d2)

    @pl.loop(0, sx + 6)
    def _(s):
        unfold(vext[s].astype(f32), 8, n1, x1.at[s])

    for a in range(3):
        for k in range(9):
            base = (27 + 9 * (2 - a) + 8 - k) * C
            kt[a, :, k * C : (k + 1) * C] = w[base : base + C]

    def conv(source, kernel, at, size, contract):
        total = None
        for a in range(3):
            lhs = source[pl.ds(at + a, size)]
            lhs = lhs.reshape(size * lhs.shape[1], L)
            term = lax.dot_general(
                lhs, kernel(a), (((1,), (contract,)), ((), ())), preferred_element_type=f32
            )
            total = term if total is None else total + term
        return total

    half = (sx + 4) // 2
    row = lax.broadcasted_iota(jnp.int32, (n1, C), 0)
    y_at = lax.div(row, 8) - 2 + gy * (ry // 8)
    y_ok = jnp.where((y_at >= 0) & (y_at < GY * (ry // 8)), 1.0, 0.0)

    @pl.loop(0, 2)
    def _(p):
        pre = conv(x1, lambda a: w[a * L : (a + 1) * L], p * half, half, 0)
        for i in range(half):
            piece = pre[i * n1 : (i + 1) * n1]
            s = p * half + i
            first[s] = piece
            x_at = s - 2 + gx * sx
            x_ok = jnp.where((x_at >= 0) & (x_at < GX * sx), 1.0, 0.0)
            hidden = gelu_value(piece).astype(bf16).astype(f32) * (y_ok * x_ok)
            unfold(hidden, 0, n2, x2.at[s])

    half2 = (sx + 2) // 2

    @pl.loop(0, 2)
    def _(p):
        pre = conv(x2, lambda a: w[27 * C + a * L : 27 * C + (a + 1) * L], p * half2, half2, 0)
        for i in range(half2):
            piece = pre[i * n2 : (i + 1) * n2]
            s = p * half2 + i
            up = cext[s].astype(f32)[8 : 8 + n2]
            delta = (up * gelu_slope(piece)).astype(bf16).astype(f32)
            unfold(delta, 0, ry, x3.at[s])

            @pl.when((s >= 1) & (s <= sx))
            def _():
                act[s - 1] = gelu_value(piece)[8 : 8 + ry].astype(bf16)
                r2 = lax.broadcasted_iota(jnp.int32, (n2, C), 0)
                inner = jnp.where((r2 >= 8) & (r2 < 8 + ry), delta, 0.0).astype(bf16)
                for a in range(3):
                    d2[s - 1 + a, :, a * C : (a + 1) * C] = inner

    def weight_grad(source, start, delta, base):
        n = delta.shape[1]
        rhs = delta[...].reshape((sx + 2) * n, 3 * C)

        @pl.loop(0, 3)
        def _(m):
            lanes = pl.ds(pl.multiple_of(m * 3 * C, C), 3 * C)
            lhs = source[pl.ds(start, sx + 2), :, lanes].reshape((sx + 2) * n, 3 * C)
            out = lax.dot_general(lhs, rhs, (((0,), (0,)), ((), ())), preferred_element_type=f32)
            for a in range(3):
                at = pl.multiple_of(base + a * L + m * 3 * C, C)
                grad[pl.ds(at, 3 * C)] = out[:, a * C : (a + 1) * C].astype(bf16)

    weight_grad(x2, 1, d2, 27 * C)

    back = conv(x3, lambda a: kt[a], 0, sx, 1)
    for i in range(sx):
        piece = back[i * ry : (i + 1) * ry]
        slope = gelu_slope(first[i + 2][16 : 16 + ry])
        delta = (piece * slope).astype(bf16)
        for a in range(3):
            d1[i + a, 16 : 16 + ry, a * C : (a + 1) * C] = delta
    weight_grad(x1, 2, d1, 0)


def reduce_kernel(counts, g, out, r1, a1, r2, a2, r3, a3, r4, fin, s1, q1, s2, q2, s3, q3, s4, q4, s5, q5, s6, q6):
    D, GX, GY = counts
    d, x, y, bx, by, bc = place()
    H = out.shape[0]
    Q = H // 4
    cut = Q // 32 * 16
    px, py, pc = (d, flip(x, bx, 1), y), (d, x, flip(y, by, 2)), (d, x, flip(y, bc, 1))
    pxy = (d, flip(x, bx, 1), flip(y, by, 2))

    barrier = pltpu.get_barrier_semaphore()
    for target in (px, py, pc, pxy):
        pl.semaphore_signal(barrier, inc=1, device_id=target, device_id_type=MESH)
    for t in range(1, D):
        pl.semaphore_signal(barrier, inc=1, device_id=(lax.rem(d + t, D), x, y), device_id_type=MESH)
    pl.semaphore_wait(barrier, 4 + D - 1)

    def copy(src, dst, send, recv, target):
        return pltpu.make_async_remote_copy(
            src_ref=src, dst_ref=dst, send_sem=send, recv_sem=recv, device_id=target, device_id_type=MESH
        )

    def quarter(s, q):
        return pl.ds(pl.multiple_of(s * H + q * Q, 16), Q)

    def stage1(s, b):
        return copy(g.at[quarter(s, 2 * b + 1 - bc)], r1.at[s, b], s1.at[s, b], q1.at[s, b], pc)

    def bits(s):
        return (bx, by, px, py) if s % 2 == 0 else (by, bx, py, px)

    def stage2(s):
        b, _, target, _ = bits(s)
        return copy(a1.at[s, 1 - b], r2.at[s], s2.at[s], q2.at[s], target)

    def halves(bit, body):
        @pl.when(bit == 0)
        def _():
            body(0, cut, cut, Q - cut)

        @pl.when(bit == 1)
        def _():
            body(cut, Q - cut, 0, cut)

    def stage3(s, lo, n):
        target = bits(s)[3]
        return copy(a2.at[s, pl.ds(lo, n)], r3.at[s, pl.ds(lo, n)], s3.at[s], q3.at[s], target)

    for s in range(D):
        for b in range(2):
            stage1(s, b).start()
    for s in range(D):
        for b in range(2):
            stage1(s, b).wait_recv()
            a1[s, b] = (g[quarter(s, 2 * b + bc)].astype(f32) + r1[s, b].astype(f32)).astype(bf16)
        stage2(s).start()
    for s in range(D):
        stage2(s).wait_recv()
        b = bits(s)[0]
        a2[s] = (a1[s, b].astype(f32) + r2[s].astype(f32)).astype(bf16)

        def send(lo, n, olo, on, s=s):
            stage3(s, olo, on).start()

        halves(bits(s)[1], send)

    def stage4(s, t, lo, n):
        return copy(a3.at[s, pl.ds(lo, n)], r4.at[t - 1, pl.ds(lo, n)], s4.at[t - 1], q4.at[t - 1], (s, x, y))

    for s in range(D):
        def add(lo, n, olo, on, s=s):
            stage3(s, lo, n).wait_recv()
            at = pl.ds(lo, n)
            a3[s, at] = (a2[s, at].astype(f32) + r3[s, at].astype(f32)).astype(bf16)
            for t in range(1, D):
                @pl.when(lax.rem(d + t, D) == s)
                def _(t=t):
                    stage4(s, t, lo, n).start()

        halves(bits(s)[1], add)

    for s in range(D):
        @pl.when(d == s)
        def _(s=s):
            b, e, partner, across = bits(s)

            def piece(fb, lo, n):
                return fin.at[pl.ds(pl.multiple_of((2 * fb + bc) * Q + lo, 16), n)]

            def share(k, fb, lo, n, target):
                return copy(piece(fb, lo, n), piece(fb, lo, n), s5.at[k], q5.at[k], target)

            targets = (partner, across, pxy)

            def finish(lo, n, olo, on):
                at = pl.ds(lo, n)
                total = a3[s, at].astype(f32)
                for t in range(1, D):
                    stage4(s, t, lo, n).wait_recv()
                    total = total + r4[t - 1, at].astype(f32)
                piece(b, lo, n)[...] = total.astype(bf16)
                for k in range(3):
                    share(k, b, lo, n, targets[k]).start()
                share(0, 1 - b, lo, n, partner).wait_recv()
                share(1, b, olo, on, across).wait_recv()
                share(2, 1 - b, olo, on, pxy).wait_recv()

            halves(e, finish)

    def stage6(b, c):
        ref = fin.at[pl.ds(pl.multiple_of((2 * b + c) * Q, 16), Q)]
        return copy(ref, ref, s6.at[b], q6.at[b], pc)

    for b in range(2):
        stage6(b, bc).start()
    for b in range(2):
        stage6(b, 1 - bc).wait_recv()
    out[...] = fin[...]

    for s in range(D):
        for b in range(2):
            stage1(s, b).wait_send()
        stage2(s).wait_send()

        def drain(lo, n, olo, on, s=s):
            stage3(s, olo, on).wait_send()
            for t in range(1, D):
                @pl.when(lax.rem(d + t, D) == s)
                def _(t=t):
                    stage4(s, t, lo, n).wait_send()

            @pl.when(d == s)
            def _():
                for k in range(3):
                    ref = fin.at[pl.ds(lo, n)]
                    copy(ref, ref, s5.at[k], q5.at[k], pc).wait_send()

        halves(bits(s)[1], drain)
    for b in range(2):
        stage6(b, bc).wait_send()


def adam_update(master, moment_one, moment_two, gradient):
    new_one = beta_one * moment_one + (1.0 - beta_one) * gradient
    new_two = beta_two * moment_two + (1.0 - beta_two) * gradient * gradient
    update = new_one / (1.0 - beta_one**10) / (jnp.sqrt(new_two / (1.0 - beta_two**10)) + epsilon)
    return (master - learn_rate * update, new_one, new_two)


def per_device(counts, volume, cotangent, master, moment_one, moment_two):
    D, GX, GY = counts
    _, sx, sy, sz, width = volume.shape
    ry = sy * sz
    H = master.shape[0]
    Q = H // 4
    sem = pltpu.SemaphoreType.DMA
    whole = pl.BlockSpec(memory_space=VMEM)
    vol = volume.reshape(sx, ry, width)
    cot = cotangent.reshape(sx, ry, width)
    vext, cext, w = pl.pallas_call(
        functools.partial(gather_kernel, counts),
        out_shape=(
            jax.ShapeDtypeStruct((sx + 2 * HX, ry + 16 * HY, width), bf16),
            jax.ShapeDtypeStruct((sx + 2, ry + 16 * CY, width), bf16),
            jax.ShapeDtypeStruct((D * H, width), bf16),
        ),
        in_specs=[whole] * 3,
        out_specs=(whole,) * 3,
        scratch_shapes=[sem((2, 8)), sem((2, 8)), sem((5, D)), sem((5, D))],
        compiler_params=pltpu.CompilerParams(
            collective_id=0, has_side_effects=True, vmem_limit_bytes=24 * 2**20
        ),
        name="gather",
    )(vol, cot, master)
    n1, n2 = ry + 32, ry + 16
    act, grad = pl.pallas_call(
        functools.partial(compute_kernel, counts),
        out_shape=(
            jax.ShapeDtypeStruct((sx, ry, width), bf16),
            jax.ShapeDtypeStruct((D * H, width), bf16),
        ),
        in_specs=[whole] * 3,
        out_specs=(whole,) * 2,
        scratch_shapes=[
            VMEM((sx + 6, n1, 9 * C), bf16),
            VMEM((sx + 4, n2, 9 * C), bf16),
            VMEM((sx + 2, ry, 9 * C), bf16),
            VMEM((sx + 4, n1, C), f32),
            VMEM((3, C, 9 * C), bf16),
            VMEM((sx + 2, n1, 3 * C), bf16),
            VMEM((sx + 2, n2, 3 * C), bf16),
        ],
        compiler_params=pltpu.CompilerParams(vmem_limit_bytes=48 * 2**20),
        name="compute",
    )(vext, cext, w)
    rows = pl.pallas_call(
        functools.partial(reduce_kernel, counts),
        out_shape=jax.ShapeDtypeStruct((H, width), bf16),
        in_specs=[whole],
        out_specs=whole,
        scratch_shapes=[
            VMEM((D, 2, Q, width), bf16),
            VMEM((D, 2, Q, width), bf16),
            VMEM((D, Q, width), bf16),
            VMEM((D, Q, width), bf16),
            VMEM((D, Q, width), bf16),
            VMEM((D, Q, width), bf16),
            VMEM((D - 1, Q, width), bf16),
            VMEM((H, width), bf16),
            sem((D, 2)), sem((D, 2)), sem((D,)), sem((D,)), sem((D,)), sem((D,)),
            sem((D - 1,)), sem((D - 1,)), sem((3,)), sem((3,)), sem((2,)), sem((2,)),
        ],
        compiler_params=pltpu.CompilerParams(
            collective_id=1, has_side_effects=True, vmem_limit_bytes=24 * 2**20
        ),
        name="reduce",
    )(grad)
    new_master, new_one, new_two = adam_update(master, moment_one, moment_two, rows.astype(f32))
    return (act.reshape(volume.shape), new_master, new_one, new_two)


def solution(mesh):
    counts = (mesh.shape["dp"], mesh.shape["gx"], mesh.shape["gy"])
    return jax.shard_map(
        functools.partial(per_device, counts),
        mesh=mesh,
        in_specs=(
            P("dp", "gx", "gy", None, None),
            P("dp", "gx", "gy", None, None),
            P("dp", None),
            P("dp", None),
            P("dp", None),
        ),
        out_specs=(P("dp", "gx", "gy", None, None), P("dp", None), P("dp", None), P("dp", None)),
        check_vma=False,
    )
```

```python
import functools

import jax
import jax.numpy as jnp
from jax import lax
from jax.experimental import pallas as pl
from jax.experimental.pallas import tpu as pltpu
from jax.sharding import PartitionSpec as P

inv_root_two = 0.7071067811865476
inv_root_tau = 0.3989422804014327
beta_one = 0.9
beta_two = 0.999
learn_rate = 0.01
epsilon = 1e-08
C = 128
HX, HY, CY = 3, 4, 2
MESH = pl.DeviceIdType.MESH
VMEM = pltpu.VMEM
f32, bf16 = jnp.float32, jnp.bfloat16


def gelu_value(field):
    return 0.5 * field * (1.0 + lax.erf(field * inv_root_two))


def gelu_slope(field):
    normal_cdf = 0.5 * (1.0 + lax.erf(field * inv_root_two))
    return normal_cdf + field * jnp.exp(-0.5 * field * field) * inv_root_tau


def place():
    d, x, y = lax.axis_index("dp"), lax.axis_index("gx"), lax.axis_index("gy")
    return d, x, y, lax.rem(x, 2), lax.rem(lax.div(y, 2), 2), lax.rem(y, 2)


def flip(index, bit, step):
    return index + step - 2 * step * bit


def gather_phases(counts, vol, cot, master_hbm, master, vext, cext, w, msem, hsend, hrecv, wsend, wrecv):
    D, GX, GY = counts
    d, x, y, bx, by, bc = place()
    sx, ry = vol.shape[0], vol.shape[1]
    H = master.shape[0]
    Q = H // 4
    N = 3
    part_rows = Q // N
    load = pltpu.make_async_copy(master_hbm, master, msem)
    load.start()
    here = {"x": (d, flip(x, bx, 1), y), "y": (d, x, flip(y, by, 2)), "c": (d, x, flip(y, bc, 1))}

    vext[...] = jnp.zeros_like(vext)
    cext[...] = jnp.zeros_like(cext)
    around = [(i, j) for i in (-1, 0, 1) for j in (-1, 0, 1) if (i, j) != (0, 0)]

    def exists(i, j):
        ok = None
        for value, step, count in ((x, i, GX), (y, j, GY)):
            if step:
                now = (value + step >= 0) & (value + step < count)
                ok = now if ok is None else ok & now
        return ok

    barrier = pltpu.get_barrier_semaphore()
    total = jnp.int32(4)
    for target in (here["x"], here["y"], here["c"], (d, here["x"][1], here["y"][2])):
        pl.semaphore_signal(barrier, inc=1, device_id=target, device_id_type=MESH)
    for i, j in around:
        ok = exists(i, j)

        @pl.when(ok)
        def _(i=i, j=j):
            pl.semaphore_signal(barrier, inc=1, device_id=(d, x + i, y + j), device_id_type=MESH)

        total = total + jnp.where(ok, 1, 0)
    for t in range(1, D):
        pl.semaphore_signal(barrier, inc=1, device_id=(lax.rem(d + t, D), x, y), device_id_type=MESH)
    total = total + (D - 1)

    vext[pl.ds(HX, sx), pl.ds(8 * HY, ry)] = vol[...]
    cext[pl.ds(1, sx), pl.ds(8 * CY, ry)] = cot[...]
    load.wait()
    w[pl.ds(pl.multiple_of(d * H, 16), H)] = master[...].astype(bf16)
    pl.semaphore_wait(barrier, total)

    def rows(s, q, n):
        return w.at[pl.ds(pl.multiple_of(s * H + q * Q + n * part_rows, 16), part_rows)]

    def move(ref, k, s, n, target):
        return pltpu.make_async_remote_copy(
            src_ref=ref, dst_ref=ref, send_sem=wsend.at[k, s, n], recv_sem=wrecv.at[k, s, n],
            device_id=target, device_id_type=MESH,
        )

    def bit(s):
        return jnp.where(lax.rem(s, 2) == 0, bx, by)

    def quarter(s):
        return 2 * bit(s) + bc

    def other(s):
        return 2 * (1 - bit(s)) + bc

    def up(s, n):
        return move(rows(s, quarter(s), n), 0, s, n, (d + 1, x, y))

    def down(s, n):
        return move(rows(s, quarter(s), n), 1, s, n, (d - 1, x, y))

    def partner(s, q, n):
        even = lax.rem(s, 2) == 0
        target = (d, jnp.where(even, here["x"][1], x), jnp.where(even, y, here["y"][2]))
        return move(rows(s, q, n), 2, s, n, target)

    def sibling(s, q, k, n):
        return move(rows(s, q, n), k, s, n, here["c"])

    @pl.when(d < D - 1)
    def _():
        for n in range(N):
            up(d, n).start()

    @pl.when(d > 0)
    def _():
        for n in range(N):
            down(d, n).start()

    def halo(n, i, j):
        def part(step, halo_x, size):
            if step < 0:
                return 0, halo_x + size, halo_x
            if step > 0:
                return size - halo_x, 0, halo_x
            return 0, halo_x, size

        copies = []
        for k, (src, dst, hx, hy) in enumerate(((vol, vext, HX, HY), (cot, cext, 1, CY))):
            xs, xd, xn = part(i, hx, sx)
            ys, yd, yn = part(j, 8 * hy, ry)
            copies.append(
                pltpu.make_async_remote_copy(
                    src_ref=src.at[pl.ds(xs, xn), pl.ds(ys, yn)],
                    dst_ref=dst.at[pl.ds(xd, xn), pl.ds(yd, yn)],
                    send_sem=hsend.at[k, n], recv_sem=hrecv.at[k, n],
                    device_id=(d, x + i, y + j), device_id_type=MESH,
                )
            )
        return copies

    for n, (i, j) in enumerate(around):
        @pl.when(exists(i, j))
        def _(n=n, i=i, j=j):
            for copy in halo(n, i, j):
                copy.start()

    def relay(t, n):
        for sign, line, more in ((-1, up, d < D - 1), (1, down, d > 0)):
            s = d + sign * t

            @pl.when((s >= 0) & (s < D))
            def _(s=s, line=line, more=more):
                line(s, n).wait_recv()

                @pl.when(more)
                def _():
                    line(s, n).start()

                partner(s, quarter(s), n).start()
                sibling(s, quarter(s), 3, n).start()

    def pass_on(t, n):
        for s in (d - t, d + t):
            @pl.when((s >= 0) & (s < D))
            def _(s=s):
                partner(s, other(s), n).wait_recv()
                sibling(s, other(s), 4, n).start()

    for n in range(N):
        relay(1, n)

    for n, (i, j) in enumerate(around):
        @pl.when(exists(i, j))
        def _(n=n, i=i, j=j):
            for copy in halo(7 - n, -i, -j):
                copy.wait_recv()

    yield

    steps = [(t, n) for t in range(1, D) for n in range(N)]
    behind = 0
    for at in range(N, len(steps)):
        relay(*steps[at])
        if at >= N:
            pass_on(*steps[behind])
            behind += 1
    for at in range(behind, len(steps)):
        pass_on(*steps[at])

    for low, high in ((0, D // 2), (D // 2, D)):
        for s in range(low, high):
            @pl.when(d != s)
            def _(s=s):
                z = jnp.int32(s)
                for n in range(N):
                    sibling(z, 2 * bit(z) + 1 - bc, 3, n).wait_recv()
                    sibling(z, 2 * (1 - bit(z)) + 1 - bc, 4, n).wait_recv()

        yield

    for s in range(D):
        z = jnp.int32(s)

        @pl.when(d != s)
        def _(z=z):
            for n in range(N):
                partner(z, quarter(z), n).wait_send()
                sibling(z, quarter(z), 3, n).wait_send()
                sibling(z, other(z), 4, n).wait_send()

        @pl.when((s <= d) & (d < D - 1))
        def _(z=z):
            for n in range(N):
                up(z, n).wait_send()

        @pl.when((s >= d) & (d > 0))
        def _(z=z):
            for n in range(N):
                down(z, n).wait_send()

    for n, (i, j) in enumerate(around):
        @pl.when(exists(i, j))
        def _(n=n, i=i, j=j):
            for copy in halo(n, i, j):
                copy.wait_send()

    yield


def shifted(field):
    rows = field.shape[0]
    z = lax.rem(lax.broadcasted_iota(jnp.int32, field.shape, 0), 8)
    before = jnp.where(z == 0, 0.0, pltpu.roll(field, 1, 0))
    after = jnp.where(z == 7, 0.0, pltpu.roll(field, rows - 1, 0))
    return before, field, after


def unfold(field, first, rows, out):
    views = shifted(field)
    for b in range(3):
        for c in range(3):
            k = 3 * b + c
            out[:, k * C : (k + 1) * C] = views[c][first + 8 * b : first + 8 * b + rows].astype(bf16)


def compute_phases(counts, vext, cext, w, act, grad, x1, x2, x3, first, kt, d1, d2):
    D, GX, GY = counts
    sx = vext.shape[0] - 2 * HX
    ry = vext.shape[1] - 16 * HY
    gx, gy = lax.axis_index("gx"), lax.axis_index("gy")
    n1, n2 = ry + 32, ry + 16
    L = 9 * C

    d1[...] = jnp.zeros_like(d1)
    d2[...] = jnp.zeros_like(d2)

    @pl.loop(0, sx + 6)
    def _(s):
        unfold(vext[s].astype(f32), 8, n1, x1.at[s])

    yield

    def conv(source, kernel, at, size, contract):
        total = None
        for a in range(3):
            lhs = source[pl.ds(at + a, size)]
            lhs = lhs.reshape(size * lhs.shape[1], L)
            term = lax.dot_general(
                lhs, kernel(a), (((1,), (contract,)), ((), ())), preferred_element_type=f32
            )
            total = term if total is None else total + term
        return total

    half = (sx + 4) // 2
    row = lax.broadcasted_iota(jnp.int32, (n1, C), 0)
    y_at = lax.div(row, 8) - 2 + gy * (ry // 8)
    y_ok = jnp.where((y_at >= 0) & (y_at < GY * (ry // 8)), 1.0, 0.0)

    @pl.loop(0, 2)
    def _(p):
        pre = conv(x1, lambda a: w[a * L : (a + 1) * L], p * half, half, 0)
        for i in range(half):
            piece = pre[i * n1 : (i + 1) * n1]
            s = p * half + i
            first[s] = piece
            x_at = s - 2 + gx * sx
            x_ok = jnp.where((x_at >= 0) & (x_at < GX * sx), 1.0, 0.0)
            hidden = gelu_value(piece).astype(bf16).astype(f32) * (y_ok * x_ok)
            unfold(hidden, 0, n2, x2.at[s])

    yield

    for a in range(3):
        for k in range(9):
            base = (27 + 9 * (2 - a) + 8 - k) * C
            kt[a, :, k * C : (k + 1) * C] = w[base : base + C]

    half2 = (sx + 2) // 2

    @pl.loop(0, 2)
    def _(p):
        pre = conv(x2, lambda a: w[27 * C + a * L : 27 * C + (a + 1) * L], p * half2, half2, 0)
        for i in range(half2):
            piece = pre[i * n2 : (i + 1) * n2]
            s = p * half2 + i
            up = cext[s].astype(f32)[8 : 8 + n2]
            delta = (up * gelu_slope(piece)).astype(bf16).astype(f32)
            unfold(delta, 0, ry, x3.at[s])

            @pl.when((s >= 1) & (s <= sx))
            def _():
                act[s - 1] = gelu_value(piece)[8 : 8 + ry].astype(bf16)
                r2 = lax.broadcasted_iota(jnp.int32, (n2, C), 0)
                inner = jnp.where((r2 >= 8) & (r2 < 8 + ry), delta, 0.0).astype(bf16)
                for a in range(3):
                    d2[s - 1 + a, :, a * C : (a + 1) * C] = inner

    def weight_grad(source, start, delta, base):
        n = delta.shape[1]
        rhs = delta[...].reshape((sx + 2) * n, 3 * C)

        @pl.loop(0, 3)
        def _(m):
            lanes = pl.ds(pl.multiple_of(m * 3 * C, C), 3 * C)
            lhs = source[pl.ds(start, sx + 2), :, lanes].reshape((sx + 2) * n, 3 * C)
            out = lax.dot_general(lhs, rhs, (((0,), (0,)), ((), ())), preferred_element_type=f32)
            for a in range(3):
                at = pl.multiple_of(base + a * L + m * 3 * C, C)
                grad[pl.ds(at, 3 * C)] = out[:, a * C : (a + 1) * C].astype(bf16)

    weight_grad(x2, 1, d2, 27 * C)
    yield

    back = conv(x3, lambda a: kt[a], 0, sx, 1)
    for i in range(sx):
        piece = back[i * ry : (i + 1) * ry]
        slope = gelu_slope(first[i + 2][16 : 16 + ry])
        delta = (piece * slope).astype(bf16)
        for a in range(3):
            d1[i + a, 16 : 16 + ry, a * C : (a + 1) * C] = delta
    yield

    weight_grad(x1, 2, d1, 0)
    yield


def reduce_phases(counts, g, out, r1, a1, r2, a2, r3, a3, r4, fin, s1, q1, s2, q2, s3, q3, s4, q4, s5, q5, s6, q6):
    D, GX, GY = counts
    d, x, y, bx, by, bc = place()
    H = out.shape[0]
    Q = H // 4
    cut = Q // 32 * 16
    px, py, pc = (d, flip(x, bx, 1), y), (d, x, flip(y, by, 2)), (d, x, flip(y, bc, 1))
    pxy = (d, flip(x, bx, 1), flip(y, by, 2))

    def copy(src, dst, send, recv, target):
        return pltpu.make_async_remote_copy(
            src_ref=src, dst_ref=dst, send_sem=send, recv_sem=recv, device_id=target, device_id_type=MESH
        )

    def quarter(s, q):
        return pl.ds(pl.multiple_of(s * H + q * Q, 16), Q)

    def stage1(s, b):
        return copy(g.at[quarter(s, 2 * b + 1 - bc)], r1.at[s, b], s1.at[s, b], q1.at[s, b], pc)

    def bits(s):
        return (bx, by, px, py) if s % 2 == 0 else (by, bx, py, px)

    def stage2(s):
        b, _, target, _ = bits(s)
        return copy(a1.at[s, 1 - b], r2.at[s], s2.at[s], q2.at[s], target)

    def halves(bit, body):
        @pl.when(bit == 0)
        def _():
            body(0, cut, cut, Q - cut)

        @pl.when(bit == 1)
        def _():
            body(cut, Q - cut, 0, cut)

    def stage3(s, lo, n):
        target = bits(s)[3]
        return copy(a2.at[s, pl.ds(lo, n)], r3.at[s, pl.ds(lo, n)], s3.at[s], q3.at[s], target)

    def begin(s):
        for b in range(2):
            stage1(s, b).start()

    def after1(s):
        for b in range(2):
            stage1(s, b).wait_recv()
            a1[s, b] = (g[quarter(s, 2 * b + bc)].astype(f32) + r1[s, b].astype(f32)).astype(bf16)
        stage2(s).start()

    def after2(s):
        stage2(s).wait_recv()
        b = bits(s)[0]
        a2[s] = (a1[s, b].astype(f32) + r2[s].astype(f32)).astype(bf16)
        halves(bits(s)[1], lambda lo, n, olo, on: stage3(s, olo, on).start())

    def stage4(s, t, lo, n):
        return copy(a3.at[s, pl.ds(lo, n)], r4.at[t - 1, pl.ds(lo, n)], s4.at[t - 1], q4.at[t - 1], (s, x, y))

    def after3(s):
        def add(lo, n, olo, on):
            stage3(s, lo, n).wait_recv()
            at = pl.ds(lo, n)
            a3[s, at] = (a2[s, at].astype(f32) + r3[s, at].astype(f32)).astype(bf16)
            for t in range(1, D):
                @pl.when(lax.rem(d + t, D) == s)
                def _(t=t):
                    stage4(s, t, lo, n).start()

        halves(bits(s)[1], add)

    early, late = range(D // 2, D), range(D // 2)
    for s in early:
        begin(s)
    yield
    for s in early:
        after1(s)
    yield
    for s in late:
        begin(s)
    for s in early:
        after2(s)
    for s in late:
        after1(s)
    for s in early:
        after3(s)
    for s in late:
        after2(s)
    for s in late:
        after3(s)

    for s in range(D):
        @pl.when(d == s)
        def _(s=s):
            b, e, partner, across = bits(s)

            def piece(fb, lo, n):
                return fin.at[pl.ds(pl.multiple_of((2 * fb + bc) * Q + lo, 16), n)]

            def share(k, fb, lo, n, target):
                return copy(piece(fb, lo, n), piece(fb, lo, n), s5.at[k], q5.at[k], target)

            targets = (partner, across, pxy)

            def finish(lo, n, olo, on):
                at = pl.ds(lo, n)
                total = a3[s, at].astype(f32)
                for t in range(1, D):
                    stage4(s, t, lo, n).wait_recv()
                    total = total + r4[t - 1, at].astype(f32)
                piece(b, lo, n)[...] = total.astype(bf16)
                for k in range(3):
                    share(k, b, lo, n, targets[k]).start()
                share(0, 1 - b, lo, n, partner).wait_recv()
                share(1, b, olo, on, across).wait_recv()
                share(2, 1 - b, olo, on, pxy).wait_recv()

            halves(e, finish)

    def stage6(b, c):
        ref = fin.at[pl.ds(pl.multiple_of((2 * b + c) * Q, 16), Q)]
        return copy(ref, ref, s6.at[b], q6.at[b], pc)

    for b in range(2):
        stage6(b, bc).start()
    for b in range(2):
        stage6(b, 1 - bc).wait_recv()
    out[...] = fin[...]

    for s in range(D):
        for b in range(2):
            stage1(s, b).wait_send()
        stage2(s).wait_send()

        def drain(lo, n, olo, on, s=s):
            stage3(s, olo, on).wait_send()
            for t in range(1, D):
                @pl.when(lax.rem(d + t, D) == s)
                def _(t=t):
                    stage4(s, t, lo, n).wait_send()

            @pl.when(d == s)
            def _():
                for k in range(3):
                    ref = fin.at[pl.ds(lo, n)]
                    copy(ref, ref, s5.at[k], q5.at[k], pc).wait_send()

        halves(bits(s)[1], drain)
    for b in range(2):
        stage6(b, bc).wait_send()
    yield


def step_kernel(counts, vol, cot, master_hbm, act, out, master, vext, cext, w, g, *scratch):
    msem, moves, fields, sums = scratch[0], scratch[1:5], scratch[5:12], scratch[12:]
    gather = gather_phases(counts, vol, cot, master_hbm, master, vext, cext, w, msem, *moves)
    compute = compute_phases(counts, vext, cext, w, act, g, *fields)
    reduce = reduce_phases(counts, g, out, *sums)
    next(gather)
    next(compute)
    next(gather)
    next(compute)
    next(gather)
    next(compute)
    next(reduce)
    next(compute)
    next(reduce)
    next(compute)
    next(reduce)
    next(gather)


def adam_update(master, moment_one, moment_two, gradient):
    new_one = beta_one * moment_one + (1.0 - beta_one) * gradient
    new_two = beta_two * moment_two + (1.0 - beta_two) * gradient * gradient
    update = new_one / (1.0 - beta_one**10) / (jnp.sqrt(new_two / (1.0 - beta_two**10)) + epsilon)
    return (master - learn_rate * update, new_one, new_two)


def per_device(counts, volume, cotangent, master, moment_one, moment_two):
    D, GX, GY = counts
    _, sx, sy, sz, width = volume.shape
    ry = sy * sz
    H = master.shape[0]
    Q = H // 4
    sem = pltpu.SemaphoreType.DMA
    whole = pl.BlockSpec(memory_space=VMEM)
    vol = volume.reshape(sx, ry, width)
    cot = cotangent.reshape(sx, ry, width)
    n1, n2 = ry + 32, ry + 16
    act, rows = pl.pallas_call(
        functools.partial(step_kernel, counts),
        out_shape=(
            jax.ShapeDtypeStruct((sx, ry, width), bf16),
            jax.ShapeDtypeStruct((H, width), bf16),
        ),
        in_specs=[whole, whole, pl.BlockSpec(memory_space=pl.ANY)],
        out_specs=(whole,) * 2,
        scratch_shapes=[
            VMEM((H, width), f32),
            VMEM((sx + 2 * HX, ry + 16 * HY, width), bf16),
            VMEM((sx + 2, ry + 16 * CY, width), bf16),
            VMEM((D * H, width), bf16),
            VMEM((D * H, width), bf16),
            sem(()), sem((2, 8)), sem((2, 8)), sem((5, D, 3)), sem((5, D, 3)),
            VMEM((sx + 6, n1, 9 * C), bf16),
            VMEM((sx + 4, n2, 9 * C), bf16),
            VMEM((sx + 2, ry, 9 * C), bf16),
            VMEM((sx + 4, n1, C), f32),
            VMEM((3, C, 9 * C), bf16),
            VMEM((sx + 2, n1, 3 * C), bf16),
            VMEM((sx + 2, n2, 3 * C), bf16),
            VMEM((D, 2, Q, width), bf16),
            VMEM((D, 2, Q, width), bf16),
            VMEM((D, Q, width), bf16),
            VMEM((D, Q, width), bf16),
            VMEM((D, Q, width), bf16),
            VMEM((D, Q, width), bf16),
            VMEM((D - 1, Q, width), bf16),
            VMEM((H, width), bf16),
            sem((D, 2)), sem((D, 2)), sem((D,)), sem((D,)), sem((D,)), sem((D,)),
            sem((D - 1,)), sem((D - 1,)), sem((3,)), sem((3,)), sem((2,)), sem((2,)),
        ],
        compiler_params=pltpu.CompilerParams(
            collective_id=0, has_side_effects=True, vmem_limit_bytes=44 * 2**20
        ),
        cost_estimate=pl.CostEstimate(flops=4 * 10**10, bytes_accessed=10**8, transcendentals=10**6),
        name="step",
    )(vol, cot, master)
    new_master, new_one, new_two = adam_update(master, moment_one, moment_two, rows.astype(f32))
    return (act.reshape(volume.shape), new_master, new_one, new_two)


def solution(mesh):
    counts = (mesh.shape["dp"], mesh.shape["gx"], mesh.shape["gy"])
    return jax.shard_map(
        functools.partial(per_device, counts),
        mesh=mesh,
        in_specs=(
            P("dp", "gx", "gy", None, None),
            P("dp", "gx", "gy", None, None),
            P("dp", None),
            P("dp", None),
            P("dp", None),
        ),
        out_specs=(P("dp", "gx", "gy", None, None), P("dp", None), P("dp", None), P("dp", None)),
        check_vma=False,
    )
```

```python
import functools

import jax
import jax.numpy as jnp
from jax import lax
from jax.experimental import pallas as pl
from jax.experimental.pallas import tpu as pltpu
from jax.sharding import PartitionSpec as P

inv_root_two = 0.7071067811865476
inv_root_tau = 0.3989422804014327
beta_one = 0.9
beta_two = 0.999
learn_rate = 0.01
epsilon = 1e-08
C = 128
HX, HY, CY = 3, 4, 2
MESH = pl.DeviceIdType.MESH
VMEM, HBM = pltpu.VMEM, pltpu.HBM
f32, bf16 = jnp.float32, jnp.bfloat16


def gelu_value(field):
    return 0.5 * field * (1.0 + lax.erf(field * inv_root_two))


def gelu_slope(field):
    normal_cdf = 0.5 * (1.0 + lax.erf(field * inv_root_two))
    return normal_cdf + field * jnp.exp(-0.5 * field * field) * inv_root_tau


def place():
    d, x, y = lax.axis_index("dp"), lax.axis_index("gx"), lax.axis_index("gy")
    return d, x, y, lax.rem(x, 2), lax.rem(lax.div(y, 2), 2), lax.rem(y, 2)


def flip(index, bit, step):
    return index + step - 2 * step * bit


def gather_phases(counts, vol, cot, master_hbm, master, vext, cext, w, msem, hsend, hrecv, wsend, wrecv):
    D, GX, GY = counts
    d, x, y, bx, by, bc = place()
    sx, ry = vol.shape[0], vol.shape[1]
    H = master.shape[0]
    Q = H // 4
    N = 3
    part_rows = Q // N
    inner = (pl.ds(HX, sx), pl.ds(8 * HY, ry)), (pl.ds(1, sx), pl.ds(8 * CY, ry))
    load = pltpu.make_async_copy(master_hbm, master, msem.at[0])
    fields = [
        pltpu.make_async_copy(vol, vext.at[inner[0]], msem.at[1]),
        pltpu.make_async_copy(cot, cext.at[inner[1]], msem.at[2]),
    ]
    load.start()
    for copy in fields:
        copy.start()
    here = {"x": (d, flip(x, bx, 1), y), "y": (d, x, flip(y, by, 2)), "c": (d, x, flip(y, bc, 1))}

    for ref, hx, hy in ((vext, HX, 8 * HY), (cext, 1, 8 * CY)):
        end = jnp.zeros((hx, *ref.shape[1:]), bf16)
        side = jnp.zeros((sx, hy, C), bf16)
        ref[:hx] = end
        ref[hx + sx :] = end
        ref[hx : hx + sx, :hy] = side
        ref[hx : hx + sx, hy + ry :] = side
    around = [(i, j) for i in (-1, 0, 1) for j in (-1, 0, 1) if (i, j) != (0, 0)]

    def exists(i, j):
        ok = None
        for value, step, count in ((x, i, GX), (y, j, GY)):
            if step:
                now = (value + step >= 0) & (value + step < count)
                ok = now if ok is None else ok & now
        return ok

    barrier = pltpu.get_barrier_semaphore()
    total = jnp.int32(4)
    for target in (here["x"], here["y"], here["c"], (d, here["x"][1], here["y"][2])):
        pl.semaphore_signal(barrier, inc=1, device_id=target, device_id_type=MESH)
    for i, j in around:
        ok = exists(i, j)

        @pl.when(ok)
        def _(i=i, j=j):
            pl.semaphore_signal(barrier, inc=1, device_id=(d, x + i, y + j), device_id_type=MESH)

        total = total + jnp.where(ok, 1, 0)
    for t in range(1, D):
        pl.semaphore_signal(barrier, inc=1, device_id=(lax.rem(d + t, D), x, y), device_id_type=MESH)
    total = total + (D - 1)

    load.wait()
    w[pl.ds(pl.multiple_of(d * H, 16), H)] = master[...].astype(bf16)
    pl.semaphore_wait(barrier, total)

    def rows(s, q, n):
        return w.at[pl.ds(pl.multiple_of(s * H + q * Q + n * part_rows, 16), part_rows)]

    def move(ref, k, s, n, target):
        return pltpu.make_async_remote_copy(
            src_ref=ref, dst_ref=ref, send_sem=wsend.at[k, s, n], recv_sem=wrecv.at[k, s, n],
            device_id=target, device_id_type=MESH,
        )

    def bit(s):
        return jnp.where(lax.rem(s, 2) == 0, bx, by)

    def quarter(s):
        return 2 * bit(s) + bc

    def other(s):
        return 2 * (1 - bit(s)) + bc

    def up(s, n):
        return move(rows(s, quarter(s), n), 0, s, n, (d + 1, x, y))

    def down(s, n):
        return move(rows(s, quarter(s), n), 1, s, n, (d - 1, x, y))

    def partner(s, q, n):
        even = lax.rem(s, 2) == 0
        target = (d, jnp.where(even, here["x"][1], x), jnp.where(even, y, here["y"][2]))
        return move(rows(s, q, n), 2, s, n, target)

    def sibling(s, q, k, n):
        return move(rows(s, q, n), k, s, n, here["c"])

    @pl.when(d < D - 1)
    def _():
        for n in range(N):
            up(d, n).start()

    @pl.when(d > 0)
    def _():
        for n in range(N):
            down(d, n).start()

    def halo(n, i, j):
        def part(step, halo_x, size):
            if step < 0:
                return 0, halo_x + size, halo_x
            if step > 0:
                return size - halo_x, 0, halo_x
            return 0, halo_x, size

        copies = []
        for k, (src, dst, hx, hy) in enumerate(((vol, vext, HX, HY), (cot, cext, 1, CY))):
            xs, xd, xn = part(i, hx, sx)
            ys, yd, yn = part(j, 8 * hy, ry)
            copies.append(
                pltpu.make_async_remote_copy(
                    src_ref=src.at[pl.ds(xs, xn), pl.ds(ys, yn)],
                    dst_ref=dst.at[pl.ds(xd, xn), pl.ds(yd, yn)],
                    send_sem=hsend.at[k, n], recv_sem=hrecv.at[k, n],
                    device_id=(d, x + i, y + j), device_id_type=MESH,
                )
            )
        return copies

    for n, (i, j) in enumerate(around):
        @pl.when(exists(i, j))
        def _(n=n, i=i, j=j):
            for copy in halo(n, i, j):
                copy.start()

    def relay(t, n):
        for sign, line, more in ((-1, up, d < D - 1), (1, down, d > 0)):
            s = d + sign * t

            @pl.when((s >= 0) & (s < D))
            def _(s=s, line=line, more=more):
                line(s, n).wait_recv()

                @pl.when(more)
                def _():
                    line(s, n).start()

                partner(s, quarter(s), n).start()
                sibling(s, quarter(s), 3, n).start()

    def pass_on(t, n):
        for s in (d - t, d + t):
            @pl.when((s >= 0) & (s < D))
            def _(s=s):
                partner(s, other(s), n).wait_recv()
                sibling(s, other(s), 4, n).start()

    for n in range(N):
        relay(1, n)

    for n, (i, j) in enumerate(around):
        @pl.when(exists(i, j))
        def _(n=n, i=i, j=j):
            for copy in halo(7 - n, -i, -j):
                copy.wait_recv()

    for copy in fields:
        copy.wait()
    yield

    steps = [(t, n) for t in range(1, D) for n in range(N)]
    behind = 0
    for at in range(N, len(steps)):
        relay(*steps[at])
        pass_on(*steps[behind])
        behind += 1
        yield
    for at in range(behind, len(steps)):
        pass_on(*steps[at])

    for low, high in ((0, D // 2), (D // 2, D)):
        for s in range(low, high):
            @pl.when(d != s)
            def _(s=s):
                z = jnp.int32(s)
                for n in range(N):
                    sibling(z, 2 * bit(z) + 1 - bc, 3, n).wait_recv()
                    sibling(z, 2 * (1 - bit(z)) + 1 - bc, 4, n).wait_recv()

        yield

    for s in range(D):
        z = jnp.int32(s)

        @pl.when(d != s)
        def _(z=z):
            for n in range(N):
                partner(z, quarter(z), n).wait_send()
                sibling(z, quarter(z), 3, n).wait_send()
                sibling(z, other(z), 4, n).wait_send()

        @pl.when((s <= d) & (d < D - 1))
        def _(z=z):
            for n in range(N):
                up(z, n).wait_send()

        @pl.when((s >= d) & (d > 0))
        def _(z=z):
            for n in range(N):
                down(z, n).wait_send()

    for n, (i, j) in enumerate(around):
        @pl.when(exists(i, j))
        def _(n=n, i=i, j=j):
            for copy in halo(n, i, j):
                copy.wait_send()

    yield


def shifted(field):
    rows = field.shape[0]
    z = lax.rem(lax.broadcasted_iota(jnp.int32, field.shape, 0), 8)
    before = jnp.where(z == 0, 0.0, pltpu.roll(field, 1, 0))
    after = jnp.where(z == 7, 0.0, pltpu.roll(field, rows - 1, 0))
    return before, field, after


def unfold(field, first, rows, out):
    views = shifted(field)
    for b in range(3):
        for c in range(3):
            k = 3 * b + c
            out[:, k * C : (k + 1) * C] = views[c][first + 8 * b : first + 8 * b + rows].astype(bf16)


def compute_phases(counts, vext, cext, w, act, grad, x1, x2, x3, first, kt, d1, d2):
    D, GX, GY = counts
    sx = vext.shape[0] - 2 * HX
    ry = vext.shape[1] - 16 * HY
    gx, gy = lax.axis_index("gx"), lax.axis_index("gy")
    n1, n2 = ry + 32, ry + 16
    L = 9 * C

    d1[...] = jnp.zeros_like(d1)
    d2[...] = jnp.zeros_like(d2)

    cuts = 3 * (D - 2)
    edges = [(sx + 6) * k // cuts for k in range(cuts + 1)]
    for low, high in zip(edges, edges[1:]):
        @pl.loop(low, high)
        def _(s):
            unfold(vext[s].astype(f32), 8, n1, x1.at[s])

        yield

    def conv(source, kernel, at, size, contract):
        total = None
        for a in range(3):
            lhs = source[pl.ds(at + a, size)]
            lhs = lhs.reshape(size * lhs.shape[1], L)
            term = lax.dot_general(
                lhs, kernel(a), (((1,), (contract,)), ((), ())), preferred_element_type=f32
            )
            total = term if total is None else total + term
        return total

    half = (sx + 4) // 2
    row = lax.broadcasted_iota(jnp.int32, (n1, C), 0)
    y_at = lax.div(row, 8) - 2 + gy * (ry // 8)
    y_ok = jnp.where((y_at >= 0) & (y_at < GY * (ry // 8)), 1.0, 0.0)

    @pl.loop(0, 2)
    def _(p):
        pre = conv(x1, lambda a: w[a * L : (a + 1) * L], p * half, half, 0)
        for i in range(half):
            piece = pre[i * n1 : (i + 1) * n1]
            s = p * half + i
            first[s] = piece
            x_at = s - 2 + gx * sx
            x_ok = jnp.where((x_at >= 0) & (x_at < GX * sx), 1.0, 0.0)
            hidden = gelu_value(piece).astype(bf16).astype(f32) * (y_ok * x_ok)
            unfold(hidden, 0, n2, x2.at[s])

    yield

    for a in range(3):
        for k in range(9):
            base = (27 + 9 * (2 - a) + 8 - k) * C
            kt[a, :, k * C : (k + 1) * C] = w[base : base + C]

    half2 = (sx + 2) // 2

    @pl.loop(0, 2)
    def _(p):
        pre = conv(x2, lambda a: w[27 * C + a * L : 27 * C + (a + 1) * L], p * half2, half2, 0)
        for i in range(half2):
            piece = pre[i * n2 : (i + 1) * n2]
            s = p * half2 + i
            up = cext[s].astype(f32)[8 : 8 + n2]
            delta = (up * gelu_slope(piece)).astype(bf16).astype(f32)
            unfold(delta, 0, ry, x3.at[s])

            @pl.when((s >= 1) & (s <= sx))
            def _():
                act[s - 1] = gelu_value(piece)[8 : 8 + ry].astype(bf16)
                r2 = lax.broadcasted_iota(jnp.int32, (n2, C), 0)
                inner = jnp.where((r2 >= 8) & (r2 < 8 + ry), delta, 0.0).astype(bf16)
                for a in range(3):
                    d2[s - 1 + a, :, a * C : (a + 1) * C] = inner

    def weight_grad(source, start, delta, base):
        n = delta.shape[1]
        rhs = delta[...].reshape((sx + 2) * n, 3 * C)

        @pl.loop(0, 3)
        def _(m):
            lanes = pl.ds(pl.multiple_of(m * 3 * C, C), 3 * C)
            lhs = source[pl.ds(start, sx + 2), :, lanes].reshape((sx + 2) * n, 3 * C)
            out = lax.dot_general(lhs, rhs, (((0,), (0,)), ((), ())), preferred_element_type=f32)
            for a in range(3):
                at = pl.multiple_of(base + a * L + m * 3 * C, C)
                grad[pl.ds(at, 3 * C)] = out[:, a * C : (a + 1) * C].astype(bf16)

    weight_grad(x2, 1, d2, 27 * C)
    yield

    back = conv(x3, lambda a: kt[a], 0, sx, 1)
    for i in range(sx):
        piece = back[i * ry : (i + 1) * ry]
        slope = gelu_slope(first[i + 2][16 : 16 + ry])
        delta = (piece * slope).astype(bf16)
        for a in range(3):
            d1[i + a, 16 : 16 + ry, a * C : (a + 1) * C] = delta
    yield

    weight_grad(x1, 2, d1, 0)
    yield


def reduce_phases(counts, g, out, r1, a1, r2, a2, r3, a3, r4, fin, s1, q1, s2, q2, s3, q3, s4, q4, s5, q5, s6, q6):
    D, GX, GY = counts
    d, x, y, bx, by, bc = place()
    H = out.shape[0]
    Q = H // 4
    cut = Q // 32 * 16
    px, py, pc = (d, flip(x, bx, 1), y), (d, x, flip(y, by, 2)), (d, x, flip(y, bc, 1))
    pxy = (d, flip(x, bx, 1), flip(y, by, 2))

    def copy(src, dst, send, recv, target):
        return pltpu.make_async_remote_copy(
            src_ref=src, dst_ref=dst, send_sem=send, recv_sem=recv, device_id=target, device_id_type=MESH
        )

    def quarter(s, q):
        return pl.ds(pl.multiple_of(s * H + q * Q, 16), Q)

    def stage1(s, b):
        return copy(g.at[quarter(s, 2 * b + 1 - bc)], r1.at[s, b], s1.at[s, b], q1.at[s, b], pc)

    def bits(s):
        return (bx, by, px, py) if s % 2 == 0 else (by, bx, py, px)

    def stage2(s):
        b, _, target, _ = bits(s)
        return copy(a1.at[s, 1 - b], r2.at[s], s2.at[s], q2.at[s], target)

    def halves(bit, body):
        @pl.when(bit == 0)
        def _():
            body(0, cut, cut, Q - cut)

        @pl.when(bit == 1)
        def _():
            body(cut, Q - cut, 0, cut)

    def stage3(s, lo, n):
        target = bits(s)[3]
        return copy(a2.at[s, pl.ds(lo, n)], r3.at[s, pl.ds(lo, n)], s3.at[s], q3.at[s], target)

    def begin(s):
        for b in range(2):
            stage1(s, b).start()

    def after1(s):
        for b in range(2):
            stage1(s, b).wait_recv()
            a1[s, b] = (g[quarter(s, 2 * b + bc)].astype(f32) + r1[s, b].astype(f32)).astype(bf16)
        stage2(s).start()

    def after2(s):
        stage2(s).wait_recv()
        b = bits(s)[0]
        a2[s] = (a1[s, b].astype(f32) + r2[s].astype(f32)).astype(bf16)
        halves(bits(s)[1], lambda lo, n, olo, on: stage3(s, olo, on).start())

    def stage4(s, t, lo, n):
        return copy(a3.at[s, pl.ds(lo, n)], r4.at[t - 1, pl.ds(lo, n)], s4.at[t - 1], q4.at[t - 1], (s, x, y))

    def after3(s):
        def add(lo, n, olo, on):
            stage3(s, lo, n).wait_recv()
            at = pl.ds(lo, n)
            a3[s, at] = (a2[s, at].astype(f32) + r3[s, at].astype(f32)).astype(bf16)
            for t in range(1, D):
                @pl.when(lax.rem(d + t, D) == s)
                def _(t=t):
                    stage4(s, t, lo, n).start()

        halves(bits(s)[1], add)

    early, late = range(D // 2, D), range(D // 2)
    for s in early:
        begin(s)
    yield
    for s in early:
        after1(s)
    yield
    for s in late:
        begin(s)
    for s in early:
        after2(s)
    for s in late:
        after1(s)
    for s in early:
        after3(s)
    for s in late:
        after2(s)
    for s in late:
        after3(s)

    for s in range(D):
        @pl.when(d == s)
        def _(s=s):
            b, e, partner, across = bits(s)

            def piece(fb, lo, n):
                return fin.at[pl.ds(pl.multiple_of((2 * fb + bc) * Q + lo, 16), n)]

            def share(k, fb, lo, n, target):
                return copy(piece(fb, lo, n), piece(fb, lo, n), s5.at[k], q5.at[k], target)

            targets = (partner, across, pxy)

            def finish(lo, n, olo, on):
                at = pl.ds(lo, n)
                total = a3[s, at].astype(f32)
                for t in range(1, D):
                    stage4(s, t, lo, n).wait_recv()
                    total = total + r4[t - 1, at].astype(f32)
                piece(b, lo, n)[...] = total.astype(bf16)
                for k in range(3):
                    share(k, b, lo, n, targets[k]).start()
                share(0, 1 - b, lo, n, partner).wait_recv()
                share(1, b, olo, on, across).wait_recv()
                share(2, 1 - b, olo, on, pxy).wait_recv()

            halves(e, finish)

    def stage6(b, c):
        ref = fin.at[pl.ds(pl.multiple_of((2 * b + c) * Q, 16), Q)]
        return copy(ref, ref, s6.at[b], q6.at[b], pc)

    for b in range(2):
        stage6(b, bc).start()
    for b in range(2):
        stage6(b, 1 - bc).wait_recv()
    out[...] = fin[...]

    for s in range(D):
        for b in range(2):
            stage1(s, b).wait_send()
        stage2(s).wait_send()

        def drain(lo, n, olo, on, s=s):
            stage3(s, olo, on).wait_send()
            for t in range(1, D):
                @pl.when(lax.rem(d + t, D) == s)
                def _(t=t):
                    stage4(s, t, lo, n).wait_send()

            @pl.when(d == s)
            def _():
                for k in range(3):
                    ref = fin.at[pl.ds(lo, n)]
                    copy(ref, ref, s5.at[k], q5.at[k], pc).wait_send()

        halves(bits(s)[1], drain)
    for b in range(2):
        stage6(b, bc).wait_send()
    yield


def step_kernel(counts, vol, cot, master_hbm, act, out, master, vext, cext, w, g, *scratch):
    msem, moves, fields, sums = scratch[0], scratch[1:5], scratch[5:12], scratch[12:]
    gather = gather_phases(counts, vol, cot, master_hbm, master, vext, cext, w, msem, *moves)
    compute = compute_phases(counts, vext, cext, w, act, g, *fields)
    reduce = reduce_phases(counts, g, out, *sums)
    next(gather)
    for _ in range(3 * (counts[0] - 2)):
        next(compute)
        next(gather)
    next(gather)
    next(compute)
    next(gather)
    next(compute)
    next(reduce)
    next(compute)
    next(reduce)
    next(compute)
    next(reduce)
    next(gather)


def finish_kernel(act_in, rows, master, one, two, act, new_master, new_one, new_two, o0, o1, o2, i0, i1, i2, sem, fsem):
    H = master.shape[0]
    parts = 4
    n = H // parts
    loads = []
    for i in range(parts):
        at = pl.ds(i * n, n)
        for k, (src, dst) in enumerate(((master, i0), (one, i1), (two, i2))):
            copy = pltpu.make_async_copy(src.at[at], dst.at[at], fsem.at[3 * i + k])
            copy.start()
            loads.append(copy)
    copies = [pltpu.make_async_copy(act_in, act, sem.at[0])]
    copies[0].start()
    for i in range(parts):
        at = pl.ds(i * n, n)
        gradient = rows[at].astype(f32)
        for copy in loads[3 * i : 3 * i + 3]:
            copy.wait()
        first = beta_one * i1[at] + (1.0 - beta_one) * gradient
        second = beta_two * i2[at] + (1.0 - beta_two) * gradient * gradient
        step = first / (1.0 - beta_one**10) / (jnp.sqrt(second / (1.0 - beta_two**10)) + epsilon)
        o1[at] = first
        o2[at] = second
        o0[at] = i0[at] - learn_rate * step
        for k, (src, dst) in enumerate(((o0, new_master), (o1, new_one), (o2, new_two))):
            copy = pltpu.make_async_copy(src.at[at], dst.at[at], sem.at[1 + 3 * i + k])
            copy.start()
            copies.append(copy)
    for copy in copies:
        copy.wait()


def per_device(counts, volume, cotangent, master, moment_one, moment_two):
    D, GX, GY = counts
    _, sx, sy, sz, width = volume.shape
    ry = sy * sz
    H = master.shape[0]
    Q = H // 4
    sem = pltpu.SemaphoreType.DMA
    whole = pl.BlockSpec(memory_space=VMEM)
    vol = volume.reshape(sx, ry, width)
    cot = cotangent.reshape(sx, ry, width)
    n1, n2 = ry + 32, ry + 16
    act, rows = pl.pallas_call(
        functools.partial(step_kernel, counts),
        out_shape=(
            jax.ShapeDtypeStruct((sx, ry, width), bf16),
            jax.ShapeDtypeStruct((H, width), bf16),
        ),
        in_specs=[pl.BlockSpec(memory_space=HBM)] * 3,
        out_specs=(whole,) * 2,
        scratch_shapes=[
            VMEM((H, width), f32),
            VMEM((sx + 2 * HX, ry + 16 * HY, width), bf16),
            VMEM((sx + 2, ry + 16 * CY, width), bf16),
            VMEM((D * H, width), bf16),
            VMEM((D * H, width), bf16),
            sem((3,)), sem((2, 8)), sem((2, 8)), sem((5, D, 3)), sem((5, D, 3)),
            VMEM((sx + 6, n1, 9 * C), bf16),
            VMEM((sx + 4, n2, 9 * C), bf16),
            VMEM((sx + 2, ry, 9 * C), bf16),
            VMEM((sx + 4, n1, C), f32),
            VMEM((3, C, 9 * C), bf16),
            VMEM((sx + 2, n1, 3 * C), bf16),
            VMEM((sx + 2, n2, 3 * C), bf16),
            VMEM((D, 2, Q, width), bf16),
            VMEM((D, 2, Q, width), bf16),
            VMEM((D, Q, width), bf16),
            VMEM((D, Q, width), bf16),
            VMEM((D, Q, width), bf16),
            VMEM((D, Q, width), bf16),
            VMEM((D - 1, Q, width), bf16),
            VMEM((H, width), bf16),
            sem((D, 2)), sem((D, 2)), sem((D,)), sem((D,)), sem((D,)), sem((D,)),
            sem((D - 1,)), sem((D - 1,)), sem((3,)), sem((3,)), sem((2,)), sem((2,)),
        ],
        compiler_params=pltpu.CompilerParams(
            collective_id=0, has_side_effects=True, vmem_limit_bytes=63 * 2**20
        ),
        cost_estimate=pl.CostEstimate(flops=4 * 10**10, bytes_accessed=10**8, transcendentals=10**6),
        name="step",
    )(vol, cot, master)
    table = jax.ShapeDtypeStruct((H, width), f32)
    act, new_master, new_one, new_two = pl.pallas_call(
        finish_kernel,
        out_shape=(jax.ShapeDtypeStruct((sx, ry, width), bf16), table, table, table),
        in_specs=[pl.BlockSpec(memory_space=pl.ANY), whole] + [pl.BlockSpec(memory_space=pl.ANY)] * 3,
        out_specs=(pl.BlockSpec(memory_space=HBM),) * 4,
        scratch_shapes=[VMEM((H, width), f32)] * 6 + [sem((13,)), sem((12,))],
        compiler_params=pltpu.CompilerParams(vmem_limit_bytes=63 * 2**20),
        name="finish",
    )(act, rows, master, moment_one, moment_two)
    return (act.reshape(volume.shape), new_master, new_one, new_two)


def solution(mesh):
    counts = (mesh.shape["dp"], mesh.shape["gx"], mesh.shape["gy"])
    return jax.shard_map(
        functools.partial(per_device, counts),
        mesh=mesh,
        in_specs=(
            P("dp", "gx", "gy", None, None),
            P("dp", "gx", "gy", None, None),
            P("dp", None),
            P("dp", None),
            P("dp", None),
        ),
        out_specs=(P("dp", "gx", "gy", None, None), P("dp", None), P("dp", None), P("dp", None)),
        check_vma=False,
    )
```

```python
import functools

import jax
import jax.numpy as jnp
from jax import lax
from jax.experimental import pallas as pl
from jax.experimental.pallas import tpu as pltpu
from jax.sharding import PartitionSpec as P

inv_root_two = 0.7071067811865476
inv_root_tau = 0.3989422804014327
beta_one = 0.9
beta_two = 0.999
learn_rate = 0.01
epsilon = 1e-08
C = 128
HX, HY, CY = 3, 4, 2
MESH = pl.DeviceIdType.MESH
VMEM, HBM = pltpu.VMEM, pltpu.HBM
f32, bf16 = jnp.float32, jnp.bfloat16


def gelu_value(field):
    return 0.5 * field * (1.0 + lax.erf(field * inv_root_two))


def gelu_slope(field):
    normal_cdf = 0.5 * (1.0 + lax.erf(field * inv_root_two))
    return normal_cdf + field * jnp.exp(-0.5 * field * field) * inv_root_tau


def place():
    d, x, y = lax.axis_index("dp"), lax.axis_index("gx"), lax.axis_index("gy")
    return d, x, y, lax.rem(x, 2), lax.rem(lax.div(y, 2), 2), lax.rem(y, 2)


def flip(index, bit, step):
    return index + step - 2 * step * bit


def gather_phases(counts, vol, cot, master_hbm, master, vext, cext, w, msem, hsend, hrecv, wsend, wrecv):
    D, GX, GY = counts
    d, x, y, bx, by, bc = place()
    sx, ry = vol.shape[0], vol.shape[1]
    H = master.shape[0]
    Q = H // 4
    N = 3
    part_rows = Q // N
    inner = (pl.ds(HX, sx), pl.ds(8 * HY, ry)), (pl.ds(1, sx), pl.ds(8 * CY, ry))
    load = pltpu.make_async_copy(master_hbm, master, msem.at[0])
    fields = [
        pltpu.make_async_copy(vol, vext.at[inner[0]], msem.at[1]),
        pltpu.make_async_copy(cot, cext.at[inner[1]], msem.at[2]),
    ]
    load.start()
    for copy in fields:
        copy.start()
    here = {"x": (d, flip(x, bx, 1), y), "y": (d, x, flip(y, by, 2)), "c": (d, x, flip(y, bc, 1))}

    for ref, hx, hy in ((vext, HX, 8 * HY), (cext, 1, 8 * CY)):
        end = jnp.zeros((hx, *ref.shape[1:]), bf16)
        side = jnp.zeros((sx, hy, C), bf16)
        ref[:hx] = end
        ref[hx + sx :] = end
        ref[hx : hx + sx, :hy] = side
        ref[hx : hx + sx, hy + ry :] = side
    around = [(i, j) for i in (-1, 0, 1) for j in (-1, 0, 1) if (i, j) != (0, 0)]

    def exists(i, j):
        ok = None
        for value, step, count in ((x, i, GX), (y, j, GY)):
            if step:
                now = (value + step >= 0) & (value + step < count)
                ok = now if ok is None else ok & now
        return ok

    barrier = pltpu.get_barrier_semaphore()
    total = jnp.int32(4)
    for target in (here["x"], here["y"], here["c"], (d, here["x"][1], here["y"][2])):
        pl.semaphore_signal(barrier, inc=1, device_id=target, device_id_type=MESH)
    for i, j in around:
        ok = exists(i, j)

        @pl.when(ok)
        def _(i=i, j=j):
            pl.semaphore_signal(barrier, inc=1, device_id=(d, x + i, y + j), device_id_type=MESH)

        total = total + jnp.where(ok, 1, 0)
    for t in range(1, D):
        pl.semaphore_signal(barrier, inc=1, device_id=(lax.rem(d + t, D), x, y), device_id_type=MESH)
    total = total + (D - 1)

    load.wait()
    w[pl.ds(pl.multiple_of(d * H, 16), H)] = master[...].astype(bf16)
    pl.semaphore_wait(barrier, total)

    def rows(s, q, n):
        return w.at[pl.ds(pl.multiple_of(s * H + q * Q + n * part_rows, 16), part_rows)]

    def move(ref, k, s, n, target):
        return pltpu.make_async_remote_copy(
            src_ref=ref, dst_ref=ref, send_sem=wsend.at[k, s, n], recv_sem=wrecv.at[k, s, n],
            device_id=target, device_id_type=MESH,
        )

    def bit(s):
        return jnp.where(lax.rem(s, 2) == 0, bx, by)

    def quarter(s):
        return 2 * bit(s) + bc

    def other(s):
        return 2 * (1 - bit(s)) + bc

    def up(s, n):
        return move(rows(s, quarter(s), n), 0, s, n, (d + 1, x, y))

    def down(s, n):
        return move(rows(s, quarter(s), n), 1, s, n, (d - 1, x, y))

    def partner(s, q, n):
        even = lax.rem(s, 2) == 0
        target = (d, jnp.where(even, here["x"][1], x), jnp.where(even, y, here["y"][2]))
        return move(rows(s, q, n), 2, s, n, target)

    def sibling(s, q, k, n):
        return move(rows(s, q, n), k, s, n, here["c"])

    @pl.when(d < D - 1)
    def _():
        for n in range(N):
            up(d, n).start()

    @pl.when(d > 0)
    def _():
        for n in range(N):
            down(d, n).start()

    def halo(n, i, j):
        def part(step, halo_x, size):
            if step < 0:
                return 0, halo_x + size, halo_x
            if step > 0:
                return size - halo_x, 0, halo_x
            return 0, halo_x, size

        copies = []
        for k, (src, dst, hx, hy) in enumerate(((vol, vext, HX, HY), (cot, cext, 1, CY))):
            xs, xd, xn = part(i, hx, sx)
            ys, yd, yn = part(j, 8 * hy, ry)
            copies.append(
                pltpu.make_async_remote_copy(
                    src_ref=src.at[pl.ds(xs, xn), pl.ds(ys, yn)],
                    dst_ref=dst.at[pl.ds(xd, xn), pl.ds(yd, yn)],
                    send_sem=hsend.at[k, n], recv_sem=hrecv.at[k, n],
                    device_id=(d, x + i, y + j), device_id_type=MESH,
                )
            )
        return copies

    for n, (i, j) in enumerate(around):
        @pl.when(exists(i, j))
        def _(n=n, i=i, j=j):
            for copy in halo(n, i, j):
                copy.start()

    def relay(t, n):
        for sign, line, more in ((-1, up, d < D - 1), (1, down, d > 0)):
            s = d + sign * t

            @pl.when((s >= 0) & (s < D))
            def _(s=s, line=line, more=more):
                line(s, n).wait_recv()

                @pl.when(more)
                def _():
                    line(s, n).start()

                partner(s, quarter(s), n).start()
                sibling(s, quarter(s), 3, n).start()

    def pass_on(t, n):
        for s in (d - t, d + t):
            @pl.when((s >= 0) & (s < D))
            def _(s=s):
                partner(s, other(s), n).wait_recv()
                sibling(s, other(s), 4, n).start()

    for n in range(N):
        relay(1, n)

    for n, (i, j) in enumerate(around):
        @pl.when(exists(i, j))
        def _(n=n, i=i, j=j):
            for copy in halo(7 - n, -i, -j):
                copy.wait_recv()

    for copy in fields:
        copy.wait()
    yield

    steps = [(t, n) for t in range(1, D) for n in range(N)]
    behind = 0
    for at in range(N, len(steps)):
        relay(*steps[at])
        pass_on(*steps[behind])
        behind += 1
        yield
    for at in range(behind, len(steps)):
        pass_on(*steps[at])

    for low, high in ((0, D // 2), (D // 2, D)):
        for s in range(low, high):
            @pl.when(d != s)
            def _(s=s):
                z = jnp.int32(s)
                for n in range(N):
                    sibling(z, 2 * bit(z) + 1 - bc, 3, n).wait_recv()
                    sibling(z, 2 * (1 - bit(z)) + 1 - bc, 4, n).wait_recv()

        yield

    for s in range(D):
        z = jnp.int32(s)

        @pl.when(d != s)
        def _(z=z):
            for n in range(N):
                partner(z, quarter(z), n).wait_send()
                sibling(z, quarter(z), 3, n).wait_send()
                sibling(z, other(z), 4, n).wait_send()

        @pl.when((s <= d) & (d < D - 1))
        def _(z=z):
            for n in range(N):
                up(z, n).wait_send()

        @pl.when((s >= d) & (d > 0))
        def _(z=z):
            for n in range(N):
                down(z, n).wait_send()

    for n, (i, j) in enumerate(around):
        @pl.when(exists(i, j))
        def _(n=n, i=i, j=j):
            for copy in halo(n, i, j):
                copy.wait_send()

    yield


def shifted(field):
    rows = field.shape[0]
    z = lax.rem(lax.broadcasted_iota(jnp.int32, field.shape, 0), 8)
    before = jnp.where(z == 0, 0.0, pltpu.roll(field, 1, 0))
    after = jnp.where(z == 7, 0.0, pltpu.roll(field, rows - 1, 0))
    return before, field, after


def unfold(field, first, rows, out):
    views = shifted(field)
    for b in range(3):
        for c in range(3):
            k = 3 * b + c
            out[:, k * C : (k + 1) * C] = views[c][first + 8 * b : first + 8 * b + rows].astype(bf16)


def compute_phases(counts, vext, cext, w, act, grad, x1, x2, x3, first, kt, d1, d2):
    D, GX, GY = counts
    sx = vext.shape[0] - 2 * HX
    ry = vext.shape[1] - 16 * HY
    gx, gy = lax.axis_index("gx"), lax.axis_index("gy")
    n1, n2 = ry + 32, ry + 16
    L = 9 * C

    d1[...] = jnp.zeros_like(d1)
    d2[...] = jnp.zeros_like(d2)

    cuts = 3 * (D - 2)
    edges = [(sx + 6) * k // cuts for k in range(cuts + 1)]
    for low, high in zip(edges, edges[1:]):
        @pl.loop(low, high)
        def _(s):
            unfold(vext[s].astype(f32), 8, n1, x1.at[s])

        yield

    def conv(source, kernel, at, size, contract):
        total = None
        for a in range(3):
            lhs = source[pl.ds(at + a, size)]
            lhs = lhs.reshape(size * lhs.shape[1], L)
            term = lax.dot_general(
                lhs, kernel(a), (((1,), (contract,)), ((), ())), preferred_element_type=f32
            )
            total = term if total is None else total + term
        return total

    half = (sx + 4) // 2
    row = lax.broadcasted_iota(jnp.int32, (n1, C), 0)
    y_at = lax.div(row, 8) - 2 + gy * (ry // 8)
    y_ok = jnp.where((y_at >= 0) & (y_at < GY * (ry // 8)), 1.0, 0.0)

    @pl.loop(0, 2)
    def _(p):
        pre = conv(x1, lambda a: w[a * L : (a + 1) * L], p * half, half, 0)
        for i in range(half):
            piece = pre[i * n1 : (i + 1) * n1]
            s = p * half + i
            first[s] = piece
            x_at = s - 2 + gx * sx
            x_ok = jnp.where((x_at >= 0) & (x_at < GX * sx), 1.0, 0.0)
            hidden = gelu_value(piece).astype(bf16).astype(f32) * (y_ok * x_ok)
            unfold(hidden, 0, n2, x2.at[s])

    yield

    for a in range(3):
        for k in range(9):
            base = (27 + 9 * (2 - a) + 8 - k) * C
            kt[a, :, k * C : (k + 1) * C] = w[base : base + C]

    half2 = (sx + 2) // 2

    @pl.loop(0, 2)
    def _(p):
        pre = conv(x2, lambda a: w[27 * C + a * L : 27 * C + (a + 1) * L], p * half2, half2, 0)
        for i in range(half2):
            piece = pre[i * n2 : (i + 1) * n2]
            s = p * half2 + i
            up = cext[s].astype(f32)[8 : 8 + n2]
            delta = (up * gelu_slope(piece)).astype(bf16).astype(f32)
            unfold(delta, 0, ry, x3.at[s])

            @pl.when((s >= 1) & (s <= sx))
            def _():
                act[s - 1] = gelu_value(piece)[8 : 8 + ry].astype(bf16)
                r2 = lax.broadcasted_iota(jnp.int32, (n2, C), 0)
                inner = jnp.where((r2 >= 8) & (r2 < 8 + ry), delta, 0.0).astype(bf16)
                for a in range(3):
                    d2[s - 1 + a, :, a * C : (a + 1) * C] = inner

    def weight_grad(source, start, delta, base):
        n = delta.shape[1]
        rhs = delta[...].reshape((sx + 2) * n, 3 * C)

        @pl.loop(0, 3)
        def _(m):
            lanes = pl.ds(pl.multiple_of(m * 3 * C, C), 3 * C)
            lhs = source[pl.ds(start, sx + 2), :, lanes].reshape((sx + 2) * n, 3 * C)
            out = lax.dot_general(lhs, rhs, (((0,), (0,)), ((), ())), preferred_element_type=f32)
            for a in range(3):
                at = pl.multiple_of(base + a * L + m * 3 * C, C)
                grad[pl.ds(at, 3 * C)] = out[:, a * C : (a + 1) * C].astype(bf16)

    weight_grad(x2, 1, d2, 27 * C)
    yield

    back = conv(x3, lambda a: kt[a], 0, sx, 1)
    for i in range(sx):
        piece = back[i * ry : (i + 1) * ry]
        slope = gelu_slope(first[i + 2][16 : 16 + ry])
        delta = (piece * slope).astype(bf16)
        for a in range(3):
            d1[i + a, 16 : 16 + ry, a * C : (a + 1) * C] = delta
    yield

    weight_grad(x1, 2, d1, 0)
    yield


def reduce_phases(counts, g, out, r1, a1, r2, a2, r3, a3, r4, fin, s1, q1, s2, q2, s3, q3, s4, q4, s5, q5, s6, q6):
    D, GX, GY = counts
    d, x, y, bx, by, bc = place()
    H = out.shape[0]
    Q = H // 4
    px, py, pc = (d, flip(x, bx, 1), y), (d, x, flip(y, by, 2)), (d, x, flip(y, bc, 1))
    pxy = (d, flip(x, bx, 1), flip(y, by, 2))
    cut = (Q // 16 + 1) // 2 * 16
    chunks = ((0, cut), (cut, Q - cut))

    def copy(src, dst, send, recv, target):
        return pltpu.make_async_remote_copy(
            src_ref=src, dst_ref=dst, send_sem=send, recv_sem=recv, device_id=target, device_id_type=MESH
        )

    def in_quarter(s, q, lo, n):
        return pl.ds(pl.multiple_of(s * H + q * Q + lo, 16), n)

    def stage1(s, b, h):
        lo, n = chunks[h]
        src = g.at[in_quarter(s, 2 * b + 1 - bc, lo, n)]
        return copy(src, r1.at[s, b, pl.ds(lo, n)], s1.at[s, b, h], q1.at[s, b, h], pc)

    def bits(s):
        return (bx, by, px, py) if s % 2 == 0 else (by, bx, py, px)

    def stage2(s, h):
        b, _, target, _ = bits(s)
        at = pl.ds(*chunks[h])
        return copy(a1.at[s, 1 - b, at], r2.at[s, at], s2.at[s, h], q2.at[s, h], target)

    def halves(bit, h, body):
        lo, n = chunks[h]
        m = n // 32 * 16

        @pl.when(bit == 0)
        def _():
            body(lo, m, lo + m, n - m)

        @pl.when(bit == 1)
        def _():
            body(lo + m, n - m, lo, m)

    def stage3(s, h, lo, n):
        at = pl.ds(lo, n)
        return copy(a2.at[s, at], r3.at[s, at], s3.at[s, h], q3.at[s, h], bits(s)[3])

    def stage4(s, t, h, lo, n):
        at = pl.ds(lo, n)
        return copy(a3.at[s, at], r4.at[t - 1, at], s4.at[t - 1, h], q4.at[t - 1, h], (s, x, y))

    def stage6(b, c, h):
        lo, n = chunks[h]
        ref = fin.at[pl.ds(pl.multiple_of((2 * b + c) * Q + lo, 16), n)]
        return copy(ref, ref, s6.at[b, h], q6.at[b, h], pc)

    def begin(s, h):
        for b in range(2):
            stage1(s, b, h).start()

    def after1(s, h):
        lo, n = chunks[h]
        at = pl.ds(lo, n)
        for b in range(2):
            stage1(s, b, h).wait_recv()
            mine = g[in_quarter(s, 2 * b + bc, lo, n)].astype(f32)
            a1[s, b, at] = (mine + r1[s, b, at].astype(f32)).astype(bf16)
        stage2(s, h).start()

    def after2(s, h):
        at = pl.ds(*chunks[h])
        stage2(s, h).wait_recv()
        b = bits(s)[0]
        a2[s, at] = (a1[s, b, at].astype(f32) + r2[s, at].astype(f32)).astype(bf16)
        halves(bits(s)[1], h, lambda lo, n, olo, on: stage3(s, h, olo, on).start())

    def after3(s, h):
        def add(lo, n, olo, on):
            stage3(s, h, lo, n).wait_recv()
            at = pl.ds(lo, n)
            a3[s, at] = (a2[s, at].astype(f32) + r3[s, at].astype(f32)).astype(bf16)
            for t in range(1, D):
                @pl.when(lax.rem(d + t, D) == s)
                def _(t=t):
                    stage4(s, t, h, lo, n).start()

        halves(bits(s)[1], h, add)

    early, late = range(D // 2, D), range(D // 2)

    def each(group, *steps):
        for fn, h in steps:
            for s in group:
                fn(s, h)

    each(early, (begin, 0), (begin, 1))
    yield
    each(early, (after1, 0), (after1, 1))
    yield
    each(late, (begin, 0), (begin, 1))
    each(early, (after2, 0), (after2, 1))
    each(late, (after1, 0))
    each(early, (after3, 0))
    each(late, (after1, 1))
    each(early, (after3, 1))
    each(late, (after2, 0), (after3, 0), (after2, 1), (after3, 1))

    for s in range(D):
        @pl.when(d == s)
        def _(s=s):
            b, e, partner, across = bits(s)

            def piece(fb, lo, n):
                return fin.at[pl.ds(pl.multiple_of((2 * fb + bc) * Q + lo, 16), n)]

            def share(k, h, fb, lo, n, target):
                return copy(piece(fb, lo, n), piece(fb, lo, n), s5.at[k, h], q5.at[k, h], target)

            targets = (partner, across, pxy)

            def total(h, lo, n):
                at = pl.ds(lo, n)
                value = a3[s, at].astype(f32)
                for t in range(1, D):
                    stage4(s, t, h, lo, n).wait_recv()
                    value = value + r4[t - 1, at].astype(f32)
                piece(b, lo, n)[...] = value.astype(bf16)
                for k in range(3):
                    share(k, h, b, lo, n, targets[k]).start()

            def collect(h, lo, n, olo, on):
                share(0, h, 1 - b, lo, n, partner).wait_recv()
                share(1, h, b, olo, on, across).wait_recv()
                share(2, h, 1 - b, olo, on, pxy).wait_recv()

            for h in range(2):
                halves(e, h, lambda lo, n, olo, on, h=h: total(h, lo, n))
            for h in range(2):
                halves(e, h, lambda lo, n, olo, on, h=h: collect(h, lo, n, olo, on))
                for fb in range(2):
                    stage6(fb, bc, h).start()

    for h in range(2):
        for b in range(2):
            stage6(b, 1 - bc, h).wait_recv()
    out[...] = fin[...]

    for s in range(D):
        for h in range(2):
            for b in range(2):
                stage1(s, b, h).wait_send()
            stage2(s, h).wait_send()

            def drain(lo, n, olo, on, s=s, h=h):
                stage3(s, h, olo, on).wait_send()
                for t in range(1, D):
                    @pl.when(lax.rem(d + t, D) == s)
                    def _(t=t):
                        stage4(s, t, h, lo, n).wait_send()

                @pl.when(d == s)
                def _():
                    for k in range(3):
                        ref = fin.at[pl.ds(lo, n)]
                        copy(ref, ref, s5.at[k, h], q5.at[k, h], pc).wait_send()

            halves(bits(s)[1], h, drain)
    for h in range(2):
        for b in range(2):
            stage6(b, bc, h).wait_send()
    yield


def step_kernel(
    counts, vol, cot, master_hbm, one_hbm, two_hbm, act, out, master, one, two, vext, cext, w, g, *scratch
):
    msem, moves, fields, sums = scratch[0], scratch[1:5], scratch[5:12], scratch[12:]
    gather = gather_phases(counts, vol, cot, master_hbm, master, vext, cext, w, msem, *moves)
    compute = compute_phases(counts, vext, cext, w, act, g, *fields)
    reduce = reduce_phases(counts, g, out, *sums)
    next(gather)
    held = [
        pltpu.make_async_copy(one_hbm, one, msem.at[3]),
        pltpu.make_async_copy(two_hbm, two, msem.at[4]),
    ]
    for copy in held:
        copy.start()
    for _ in range(3 * (counts[0] - 2)):
        next(compute)
        next(gather)
    next(gather)
    next(compute)
    next(gather)
    next(compute)
    next(reduce)
    next(compute)
    next(reduce)
    next(compute)
    next(reduce)
    next(gather)
    for copy in held:
        copy.wait()


def finish_kernel(act_in, rows, master, one, two, act, new_master, new_one, new_two, o0, o1, o2, sem):
    H = master.shape[0]
    parts = 4
    n = H // parts
    copies = [pltpu.make_async_copy(act_in, act, sem.at[0])]
    copies[0].start()
    for i in range(parts):
        at = pl.ds(i * n, n)
        gradient = rows[at].astype(f32)
        first = beta_one * one[at] + (1.0 - beta_one) * gradient
        second = beta_two * two[at] + (1.0 - beta_two) * gradient * gradient
        o1[at] = first
        o2[at] = second
        step = first / (1.0 - beta_one**10) / (jnp.sqrt(second / (1.0 - beta_two**10)) + epsilon)
        o0[at] = master[at] - learn_rate * step
        for k, (src, dst) in enumerate(((o1, new_one), (o2, new_two), (o0, new_master))):
            copy = pltpu.make_async_copy(src.at[at], dst.at[at], sem.at[1 + 3 * i + k])
            copy.start()
            copies.append(copy)
    for copy in copies:
        copy.wait()


def per_device(counts, volume, cotangent, master, moment_one, moment_two):
    D, GX, GY = counts
    _, sx, sy, sz, width = volume.shape
    ry = sy * sz
    H = master.shape[0]
    Q = H // 4
    sem = pltpu.SemaphoreType.DMA
    whole = pl.BlockSpec(memory_space=VMEM)
    vol = volume.reshape(sx, ry, width)
    cot = cotangent.reshape(sx, ry, width)
    n1, n2 = ry + 32, ry + 16
    table = jax.ShapeDtypeStruct((H, width), f32)
    act, rows, *held = pl.pallas_call(
        functools.partial(step_kernel, counts),
        out_shape=(
            jax.ShapeDtypeStruct((sx, ry, width), bf16),
            jax.ShapeDtypeStruct((H, width), bf16),
            table,
            table,
            table,
        ),
        in_specs=[pl.BlockSpec(memory_space=HBM)] * 5,
        out_specs=(whole,) * 5,
        scratch_shapes=[
            VMEM((sx + 2 * HX, ry + 16 * HY, width), bf16),
            VMEM((sx + 2, ry + 16 * CY, width), bf16),
            VMEM((D * H, width), bf16),
            VMEM((D * H, width), bf16),
            sem((5,)), sem((2, 8)), sem((2, 8)), sem((5, D, 3)), sem((5, D, 3)),
            VMEM((sx + 6, n1, 9 * C), bf16),
            VMEM((sx + 4, n2, 9 * C), bf16),
            VMEM((sx + 2, ry, 9 * C), bf16),
            VMEM((sx + 4, n1, C), f32),
            VMEM((3, C, 9 * C), bf16),
            VMEM((sx + 2, n1, 3 * C), bf16),
            VMEM((sx + 2, n2, 3 * C), bf16),
            VMEM((D, 2, Q, width), bf16),
            VMEM((D, 2, Q, width), bf16),
            VMEM((D, Q, width), bf16),
            VMEM((D, Q, width), bf16),
            VMEM((D, Q, width), bf16),
            VMEM((D, Q, width), bf16),
            VMEM((D - 1, Q, width), bf16),
            VMEM((H, width), bf16),
            sem((D, 2, 2)), sem((D, 2, 2)), sem((D, 2)), sem((D, 2)), sem((D, 2)), sem((D, 2)),
            sem((D - 1, 2)), sem((D - 1, 2)), sem((3, 2)), sem((3, 2)), sem((2, 2)), sem((2, 2)),
        ],
        compiler_params=pltpu.CompilerParams(
            collective_id=0, has_side_effects=True, vmem_limit_bytes=50 * 2**20
        ),
        cost_estimate=pl.CostEstimate(flops=4 * 10**10, bytes_accessed=10**8, transcendentals=10**6),
        name="step",
    )(vol, cot, master, moment_one, moment_two)
    act, new_master, new_one, new_two = pl.pallas_call(
        finish_kernel,
        out_shape=(jax.ShapeDtypeStruct((sx, ry, width), bf16), table, table, table),
        in_specs=[whole] * 5,
        out_specs=(pl.BlockSpec(memory_space=HBM),) * 4,
        scratch_shapes=[VMEM((H, width), f32)] * 3 + [sem((13,))],
        compiler_params=pltpu.CompilerParams(vmem_limit_bytes=8 * 2**20),
        name="finish",
    )(act, rows, *held)
    return (act.reshape(volume.shape), new_master, new_one, new_two)


def solution(mesh):
    counts = (mesh.shape["dp"], mesh.shape["gx"], mesh.shape["gy"])
    return jax.shard_map(
        functools.partial(per_device, counts),
        mesh=mesh,
        in_specs=(
            P("dp", "gx", "gy", None, None),
            P("dp", "gx", "gy", None, None),
            P("dp", None),
            P("dp", None),
            P("dp", None),
        ),
        out_specs=(P("dp", "gx", "gy", None, None), P("dp", None), P("dp", None), P("dp", None)),
        check_vma=False,
    )
```

```python
import functools

import jax
import jax.numpy as jnp
from jax import lax
from jax.experimental import pallas as pl
from jax.experimental.pallas import tpu as pltpu
from jax.sharding import PartitionSpec as P

inv_root_two = 0.7071067811865476
inv_root_tau = 0.3989422804014327
beta_one = 0.9
beta_two = 0.999
learn_rate = 0.01
epsilon = 1e-08
C = 128
HX, HY, CY = 3, 4, 2
MESH = pl.DeviceIdType.MESH
VMEM, HBM = pltpu.VMEM, pltpu.HBM
f32, bf16 = jnp.float32, jnp.bfloat16


def gelu_value(field):
    return 0.5 * field * (1.0 + lax.erf(field * inv_root_two))


def gelu_slope(field):
    normal_cdf = 0.5 * (1.0 + lax.erf(field * inv_root_two))
    return normal_cdf + field * jnp.exp(-0.5 * field * field) * inv_root_tau


def place():
    d, x, y = lax.axis_index("dp"), lax.axis_index("gx"), lax.axis_index("gy")
    return d, x, y, lax.rem(x, 2), lax.rem(lax.div(y, 2), 2), lax.rem(y, 2)


def flip(index, bit, step):
    return index + step - 2 * step * bit


def gather_phases(counts, vol, cot, master_hbm, master, vext, cext, w, msem, hsend, hrecv, wsend, wrecv):
    D, GX, GY = counts
    d, x, y, bx, by, bc = place()
    sx, ry = vol.shape[0], vol.shape[1]
    H = master.shape[0]
    Q = H // 4
    N = 3
    part_rows = Q // N
    inner = (pl.ds(HX, sx), pl.ds(8 * HY, ry)), (pl.ds(1, sx), pl.ds(8 * CY, ry))
    load = pltpu.make_async_copy(master_hbm, master, msem.at[0])
    fields = [
        pltpu.make_async_copy(vol, vext.at[inner[0]], msem.at[1]),
        pltpu.make_async_copy(cot, cext.at[inner[1]], msem.at[2]),
    ]
    load.start()
    for copy in fields:
        copy.start()
    here = {"x": (d, flip(x, bx, 1), y), "y": (d, x, flip(y, by, 2)), "c": (d, x, flip(y, bc, 1))}

    for ref, hx, hy in ((vext, HX, 8 * HY), (cext, 1, 8 * CY)):
        end = jnp.zeros((hx, *ref.shape[1:]), bf16)
        side = jnp.zeros((sx, hy, C), bf16)
        ref[:hx] = end
        ref[hx + sx :] = end
        ref[hx : hx + sx, :hy] = side
        ref[hx : hx + sx, hy + ry :] = side
    around = [(i, j) for i in (-1, 0, 1) for j in (-1, 0, 1) if (i, j) != (0, 0)]

    def exists(i, j):
        ok = None
        for value, step, count in ((x, i, GX), (y, j, GY)):
            if step:
                now = (value + step >= 0) & (value + step < count)
                ok = now if ok is None else ok & now
        return ok

    barrier = pltpu.get_barrier_semaphore()
    total = jnp.int32(4)
    for target in (here["x"], here["y"], here["c"], (d, here["x"][1], here["y"][2])):
        pl.semaphore_signal(barrier, inc=1, device_id=target, device_id_type=MESH)
    for i, j in around:
        ok = exists(i, j)

        @pl.when(ok)
        def _(i=i, j=j):
            pl.semaphore_signal(barrier, inc=1, device_id=(d, x + i, y + j), device_id_type=MESH)

        total = total + jnp.where(ok, 1, 0)
    for t in range(1, D):
        pl.semaphore_signal(barrier, inc=1, device_id=(lax.rem(d + t, D), x, y), device_id_type=MESH)
    total = total + (D - 1)

    load.wait()
    w[pl.ds(pl.multiple_of(d * H, 16), H)] = master[...].astype(bf16)
    pl.semaphore_wait(barrier, total)

    def rows(s, q, n):
        return w.at[pl.ds(pl.multiple_of(s * H + q * Q + n * part_rows, 16), part_rows)]

    def move(ref, k, s, n, target):
        return pltpu.make_async_remote_copy(
            src_ref=ref, dst_ref=ref, send_sem=wsend.at[k, s, n], recv_sem=wrecv.at[k, s, n],
            device_id=target, device_id_type=MESH,
        )

    def bit(s):
        return jnp.where(lax.rem(s, 2) == 0, bx, by)

    def quarter(s):
        return 2 * bit(s) + bc

    def other(s):
        return 2 * (1 - bit(s)) + bc

    def up(s, n):
        return move(rows(s, quarter(s), n), 0, s, n, (d + 1, x, y))

    def down(s, n):
        return move(rows(s, quarter(s), n), 1, s, n, (d - 1, x, y))

    def partner(s, q, n):
        even = lax.rem(s, 2) == 0
        target = (d, jnp.where(even, here["x"][1], x), jnp.where(even, y, here["y"][2]))
        return move(rows(s, q, n), 2, s, n, target)

    def sibling(s, q, k, n):
        return move(rows(s, q, n), k, s, n, here["c"])

    @pl.when(d < D - 1)
    def _():
        for n in range(N):
            up(d, n).start()

    @pl.when(d > 0)
    def _():
        for n in range(N):
            down(d, n).start()

    def halo(n, i, j):
        def part(step, halo_x, size):
            if step < 0:
                return 0, halo_x + size, halo_x
            if step > 0:
                return size - halo_x, 0, halo_x
            return 0, halo_x, size

        copies = []
        for k, (src, dst, hx, hy) in enumerate(((vol, vext, HX, HY), (cot, cext, 1, CY))):
            xs, xd, xn = part(i, hx, sx)
            ys, yd, yn = part(j, 8 * hy, ry)
            copies.append(
                pltpu.make_async_remote_copy(
                    src_ref=src.at[pl.ds(xs, xn), pl.ds(ys, yn)],
                    dst_ref=dst.at[pl.ds(xd, xn), pl.ds(yd, yn)],
                    send_sem=hsend.at[k, n], recv_sem=hrecv.at[k, n],
                    device_id=(d, x + i, y + j), device_id_type=MESH,
                )
            )
        return copies

    for n, (i, j) in enumerate(around):
        @pl.when(exists(i, j))
        def _(n=n, i=i, j=j):
            for copy in halo(n, i, j):
                copy.start()

    def relay(t, n):
        for sign, line, more in ((-1, up, d < D - 1), (1, down, d > 0)):
            s = d + sign * t

            @pl.when((s >= 0) & (s < D))
            def _(s=s, line=line, more=more):
                line(s, n).wait_recv()

                @pl.when(more)
                def _():
                    line(s, n).start()

                partner(s, quarter(s), n).start()
                sibling(s, quarter(s), 3, n).start()

    def pass_on(t, n):
        for s in (d - t, d + t):
            @pl.when((s >= 0) & (s < D))
            def _(s=s):
                partner(s, other(s), n).wait_recv()
                sibling(s, other(s), 4, n).start()

    for n in range(N):
        relay(1, n)

    for n, (i, j) in enumerate(around):
        @pl.when(exists(i, j))
        def _(n=n, i=i, j=j):
            for copy in halo(7 - n, -i, -j):
                copy.wait_recv()

    for copy in fields:
        copy.wait()
    yield

    def settle(low, high):
        for s in range(low, high):
            @pl.when(d != s)
            def _(s=s):
                z = jnp.int32(s)
                for n in range(N):
                    sibling(z, 2 * bit(z) + 1 - bc, 3, n).wait_recv()
                    sibling(z, 2 * (1 - bit(z)) + 1 - bc, 4, n).wait_recv()

    for n in range(N):
        relay(2, n)
        pass_on(1, n)
        yield
    yield settle
    for t in range(3, D):
        for n in range(N):
            relay(t, n)
            pass_on(t - 1, n)
    for n in range(N):
        pass_on(D - 1, n)
    yield

    for s in range(D):
        z = jnp.int32(s)

        @pl.when(d != s)
        def _(z=z):
            for n in range(N):
                partner(z, quarter(z), n).wait_send()
                sibling(z, quarter(z), 3, n).wait_send()
                sibling(z, other(z), 4, n).wait_send()

        @pl.when((s <= d) & (d < D - 1))
        def _(z=z):
            for n in range(N):
                up(z, n).wait_send()

        @pl.when((s >= d) & (d > 0))
        def _(z=z):
            for n in range(N):
                down(z, n).wait_send()

    for n, (i, j) in enumerate(around):
        @pl.when(exists(i, j))
        def _(n=n, i=i, j=j):
            for copy in halo(n, i, j):
                copy.wait_send()

    yield


def shifted(field):
    rows = field.shape[0]
    z = lax.rem(lax.broadcasted_iota(jnp.int32, field.shape, 0), 8)
    before = jnp.where(z == 0, 0.0, pltpu.roll(field, 1, 0))
    after = jnp.where(z == 7, 0.0, pltpu.roll(field, rows - 1, 0))
    return before, field, after


def unfold(field, first, rows, out):
    views = shifted(field)
    for b in range(3):
        for c in range(3):
            k = 3 * b + c
            out[:, k * C : (k + 1) * C] = views[c][first + 8 * b : first + 8 * b + rows].astype(bf16)


def compute_phases(counts, vext, cext, w, act, grad, x1, x2, x3, first, kt, kk, d1, d2):
    D, GX, GY = counts
    sx = vext.shape[0] - 2 * HX
    ry = vext.shape[1] - 16 * HY
    gx, gy = lax.axis_index("gx"), lax.axis_index("gy")
    n1, n2 = ry + 32, ry + 16
    L = 9 * C

    d1[...] = jnp.zeros_like(d1)
    d2[...] = jnp.zeros_like(d2)

    cuts = 3
    edges = [(sx + 6) * k // cuts for k in range(cuts + 1)]
    for low, high in zip(edges, edges[1:]):
        @pl.loop(low, high)
        def _(s):
            unfold(vext[s].astype(f32), 8, n1, x1.at[s])

        yield

    def conv(source, pair, last, at, size, contract):
        def product(begin, slices, kernel):
            lhs = source[pl.ds(begin, slices)].reshape(slices * source.shape[1], L)
            return lax.dot_general(
                lhs, kernel, (((1,), (contract,)), ((), ())), preferred_element_type=f32
            )

        n = source.shape[1]
        both = product(at, size + 1, pair)
        return both[: size * n, :C] + both[n:, C:] + product(at + 2, size, last)

    def load_pair(base):
        for a in range(2):
            kk[:, a * C : (a + 1) * C] = w[base + a * L : base + (a + 1) * L]

    half = (sx + 4) // 2
    row = lax.broadcasted_iota(jnp.int32, (n1, C), 0)
    y_at = lax.div(row, 8) - 2 + gy * (ry // 8)
    y_ok = jnp.where((y_at >= 0) & (y_at < GY * (ry // 8)), 1.0, 0.0)

    def first_layer():
        load_pair(0)

        @pl.loop(0, 2)
        def _(p):
            pre = conv(x1, kk[...], w[2 * L : 3 * L], p * half, half, 0)
            for i in range(half):
                piece = pre[i * n1 : (i + 1) * n1]
                s = p * half + i
                first[s] = piece
                x_at = s - 2 + gx * sx
                x_ok = jnp.where((x_at >= 0) & (x_at < GX * sx), 1.0, 0.0)
                hidden = gelu_value(piece).astype(bf16).astype(f32) * (y_ok * x_ok)
                unfold(hidden, 0, n2, x2.at[s])

    yield first_layer

    for a in range(3):
        for k in range(9):
            base = (27 + 9 * (2 - a) + 8 - k) * C
            kt[a, :, k * C : (k + 1) * C] = w[base : base + C]

    half2 = (sx + 2) // 2
    load_pair(27 * C)

    @pl.loop(0, 2)
    def _(p):
        pre = conv(x2, kk[...], w[27 * C + 2 * L : 27 * C + 3 * L], p * half2, half2, 0)
        for i in range(half2):
            piece = pre[i * n2 : (i + 1) * n2]
            s = p * half2 + i
            up = cext[s].astype(f32)[8 : 8 + n2]
            delta = (up * gelu_slope(piece)).astype(bf16).astype(f32)
            unfold(delta, 0, ry, x3.at[s])

            @pl.when((s >= 1) & (s <= sx))
            def _():
                act[s - 1] = gelu_value(piece)[8 : 8 + ry].astype(bf16)
                r2 = lax.broadcasted_iota(jnp.int32, (n2, C), 0)
                inner = jnp.where((r2 >= 8) & (r2 < 8 + ry), delta, 0.0).astype(bf16)
                for a in range(3):
                    d2[s - 1 + a, :, a * C : (a + 1) * C] = inner

    def weight_grad(source, start, delta, base):
        n = delta.shape[1]
        rhs = delta[...].reshape((sx + 2) * n, 3 * C)

        @pl.loop(0, 3)
        def _(m):
            lanes = pl.ds(pl.multiple_of(m * 3 * C, C), 3 * C)
            lhs = source[pl.ds(start, sx + 2), :, lanes].reshape((sx + 2) * n, 3 * C)
            out = lax.dot_general(lhs, rhs, (((0,), (0,)), ((), ())), preferred_element_type=f32)
            for a in range(3):
                at = pl.multiple_of(base + a * L + m * 3 * C, C)
                grad[pl.ds(at, 3 * C)] = out[:, a * C : (a + 1) * C].astype(bf16)

    weight_grad(x2, 1, d2, 27 * C)
    yield

    back = conv(x3, kt[0:2].reshape(2 * C, L), kt[2], 0, sx, 1)
    for i in range(sx):
        piece = back[i * ry : (i + 1) * ry]
        slope = gelu_slope(first[i + 2][16 : 16 + ry])
        delta = (piece * slope).astype(bf16)
        for a in range(3):
            d1[i + a, 16 : 16 + ry, a * C : (a + 1) * C] = delta
    yield

    weight_grad(x1, 2, d1, 0)
    yield


def reduce_phases(counts, g, out, r1, a1, r2, a2, r3, a3, r4, fin, s1, q1, s2, q2, s3, q3, s4, q4, s5, q5, s6, q6):
    D, GX, GY = counts
    d, x, y, bx, by, bc = place()
    H = out.shape[0]
    Q = H // 4
    px, py, pc = (d, flip(x, bx, 1), y), (d, x, flip(y, by, 2)), (d, x, flip(y, bc, 1))
    pxy = (d, flip(x, bx, 1), flip(y, by, 2))
    cut = (Q // 16 + 1) // 2 * 16
    chunks = ((0, cut), (cut, Q - cut))

    def copy(src, dst, send, recv, target):
        return pltpu.make_async_remote_copy(
            src_ref=src, dst_ref=dst, send_sem=send, recv_sem=recv, device_id=target, device_id_type=MESH
        )

    def in_quarter(s, q, lo, n):
        return pl.ds(pl.multiple_of(s * H + q * Q + lo, 16), n)

    def stage1(s, b, h):
        lo, n = chunks[h]
        src = g.at[in_quarter(s, 2 * b + 1 - bc, lo, n)]
        return copy(src, r1.at[s, b, pl.ds(lo, n)], s1.at[s, b, h], q1.at[s, b, h], pc)

    def bits(s):
        return (bx, by, px, py) if s % 2 == 0 else (by, bx, py, px)

    def stage2(s, h):
        b, _, target, _ = bits(s)
        at = pl.ds(*chunks[h])
        return copy(a1.at[s, 1 - b, at], r2.at[s, at], s2.at[s, h], q2.at[s, h], target)

    def halves(bit, h, body):
        lo, n = chunks[h]
        m = n // 32 * 16

        @pl.when(bit == 0)
        def _():
            body(lo, m, lo + m, n - m)

        @pl.when(bit == 1)
        def _():
            body(lo + m, n - m, lo, m)

    def stage3(s, h, lo, n):
        at = pl.ds(lo, n)
        return copy(a2.at[s, at], r3.at[s, at], s3.at[s, h], q3.at[s, h], bits(s)[3])

    def stage4(s, t, h, lo, n):
        at = pl.ds(lo, n)
        return copy(a3.at[s, at], r4.at[t - 1, at], s4.at[t - 1, h], q4.at[t - 1, h], (s, x, y))

    def stage6(b, c, h):
        lo, n = chunks[h]
        ref = fin.at[pl.ds(pl.multiple_of((2 * b + c) * Q + lo, 16), n)]
        return copy(ref, ref, s6.at[b, h], q6.at[b, h], pc)

    def begin(s, h):
        for b in range(2):
            stage1(s, b, h).start()

    def after1(s, h):
        lo, n = chunks[h]
        at = pl.ds(lo, n)
        for b in range(2):
            stage1(s, b, h).wait_recv()
            mine = g[in_quarter(s, 2 * b + bc, lo, n)].astype(f32)
            a1[s, b, at] = (mine + r1[s, b, at].astype(f32)).astype(bf16)
        stage2(s, h).start()

    def after2(s, h):
        at = pl.ds(*chunks[h])
        stage2(s, h).wait_recv()
        b = bits(s)[0]
        a2[s, at] = (a1[s, b, at].astype(f32) + r2[s, at].astype(f32)).astype(bf16)
        halves(bits(s)[1], h, lambda lo, n, olo, on: stage3(s, h, olo, on).start())

    def after3(s, h):
        def add(lo, n, olo, on):
            stage3(s, h, lo, n).wait_recv()
            at = pl.ds(lo, n)
            a3[s, at] = (a2[s, at].astype(f32) + r3[s, at].astype(f32)).astype(bf16)
            for t in range(1, D):
                @pl.when(lax.rem(d + t, D) == s)
                def _(t=t):
                    stage4(s, t, h, lo, n).start()

        halves(bits(s)[1], h, add)

    early, late = range(D // 2, D), range(D // 2)

    def each(group, *steps):
        for fn, h in steps:
            for s in group:
                fn(s, h)

    each(early, (begin, 0), (begin, 1))
    yield
    each(early, (after1, 0), (after1, 1))
    yield
    each(late, (begin, 0), (begin, 1))
    yield
    each(early, (after2, 0), (after2, 1))
    each(late, (after1, 0))
    each(early, (after3, 0))
    each(late, (after1, 1))
    each(early, (after3, 1))
    each(late, (after2, 0), (after3, 0), (after2, 1), (after3, 1))

    for s in range(D):
        for h in range(2):
            for b in range(2):
                stage1(s, b, h).wait_send()
            stage2(s, h).wait_send()
            halves(bits(s)[1], h, lambda lo, n, olo, on, s=s, h=h: stage3(s, h, olo, on).wait_send())

    for s in range(D):
        @pl.when(d == s)
        def _(s=s):
            b, e, partner, across = bits(s)

            def piece(fb, lo, n):
                return fin.at[pl.ds(pl.multiple_of((2 * fb + bc) * Q + lo, 16), n)]

            def share(k, h, fb, lo, n, target):
                return copy(piece(fb, lo, n), piece(fb, lo, n), s5.at[k, h], q5.at[k, h], target)

            targets = (partner, across, pxy)

            def total(h, lo, n):
                at = pl.ds(lo, n)
                value = a3[s, at].astype(f32)
                for t in range(1, D):
                    stage4(s, t, h, lo, n).wait_recv()
                    value = value + r4[t - 1, at].astype(f32)
                piece(b, lo, n)[...] = value.astype(bf16)
                for k in range(3):
                    share(k, h, b, lo, n, targets[k]).start()

            def collect(h, lo, n, olo, on):
                share(0, h, 1 - b, lo, n, partner).wait_recv()
                share(1, h, b, olo, on, across).wait_recv()
                share(2, h, 1 - b, olo, on, pxy).wait_recv()

            for h in range(2):
                halves(e, h, lambda lo, n, olo, on, h=h: total(h, lo, n))
            for h in range(2):
                halves(e, h, lambda lo, n, olo, on, h=h: collect(h, lo, n, olo, on))
                for fb in range(2):
                    stage6(fb, bc, h).start()

    for s in range(D):
        for h in range(2):
            def drain(lo, n, olo, on, s=s, h=h):
                for t in range(1, D):
                    @pl.when(lax.rem(d + t, D) == s)
                    def _(t=t):
                        stage4(s, t, h, lo, n).wait_send()

                @pl.when(d == s)
                def _():
                    for k in range(3):
                        ref = fin.at[pl.ds(lo, n)]
                        copy(ref, ref, s5.at[k, h], q5.at[k, h], pc).wait_send()

            halves(bits(s)[1], h, drain)

    for h in range(2):
        for b in range(2):
            stage6(b, 1 - bc, h).wait_recv()
    out[...] = fin[...]

    for h in range(2):
        for b in range(2):
            stage6(b, bc, h).wait_send()
    yield


def step_kernel(
    counts, vol, cot, master_hbm, one_hbm, two_hbm, act, out, master, one, two, vext, cext, w, g, *scratch
):
    msem, moves, fields, sums = scratch[0], scratch[1:5], scratch[5:13], scratch[13:]
    gather = gather_phases(counts, vol, cot, master_hbm, master, vext, cext, w, msem, *moves)
    compute = compute_phases(counts, vext, cext, w, act, g, *fields)
    reduce = reduce_phases(counts, g, out, *sums)
    next(gather)
    held = [
        pltpu.make_async_copy(one_hbm, one, msem.at[3]),
        pltpu.make_async_copy(two_hbm, two, msem.at[4]),
    ]
    for copy in held:
        copy.start()
    for _ in range(3):
        next(compute)
        next(gather)
    settle = next(gather)
    first_layer = next(compute)
    D = counts[0]
    low = lax.axis_index("dp") < D // 2

    @pl.when(low)
    def _():
        settle(0, D // 2)
        first_layer()

    next(gather)

    @pl.when(jnp.logical_not(low))
    def _():
        settle(0, D // 2)
        first_layer()

    settle(D // 2, D)
    next(compute)
    next(reduce)
    next(compute)
    next(reduce)
    next(compute)
    next(reduce)
    next(gather)
    next(reduce)
    for copy in held:
        copy.wait()


def finish_kernel(act_in, rows, master, one, two, act, new_master, new_one, new_two, o0, o1, o2, sem):
    H = master.shape[0]
    parts = 4
    n = H // parts
    copies = [pltpu.make_async_copy(act_in, act, sem.at[0])]
    copies[0].start()
    for i in range(parts):
        at = pl.ds(i * n, n)
        gradient = rows[at].astype(f32)
        first = beta_one * one[at] + (1.0 - beta_one) * gradient
        second = beta_two * two[at] + (1.0 - beta_two) * gradient * gradient
        o1[at] = first
        o2[at] = second
        step = first / (1.0 - beta_one**10) / (jnp.sqrt(second / (1.0 - beta_two**10)) + epsilon)
        o0[at] = master[at] - learn_rate * step
        for k, (src, dst) in enumerate(((o1, new_one), (o2, new_two), (o0, new_master))):
            copy = pltpu.make_async_copy(src.at[at], dst.at[at], sem.at[1 + 3 * i + k])
            copy.start()
            copies.append(copy)
    for copy in copies:
        copy.wait()


def per_device(counts, volume, cotangent, master, moment_one, moment_two):
    D, GX, GY = counts
    _, sx, sy, sz, width = volume.shape
    ry = sy * sz
    H = master.shape[0]
    Q = H // 4
    sem = pltpu.SemaphoreType.DMA
    whole = pl.BlockSpec(memory_space=VMEM)
    vol = volume.reshape(sx, ry, width)
    cot = cotangent.reshape(sx, ry, width)
    n1, n2 = ry + 32, ry + 16
    table = jax.ShapeDtypeStruct((H, width), f32)
    act, rows, *held = pl.pallas_call(
        functools.partial(step_kernel, counts),
        out_shape=(
            jax.ShapeDtypeStruct((sx, ry, width), bf16),
            jax.ShapeDtypeStruct((H, width), bf16),
            table,
            table,
            table,
        ),
        in_specs=[pl.BlockSpec(memory_space=HBM)] * 5,
        out_specs=(whole,) * 5,
        scratch_shapes=[
            VMEM((sx + 2 * HX, ry + 16 * HY, width), bf16),
            VMEM((sx + 2, ry + 16 * CY, width), bf16),
            VMEM((D * H, width), bf16),
            VMEM((D * H, width), bf16),
            sem((5,)), sem((2, 8)), sem((2, 8)), sem((5, D, 3)), sem((5, D, 3)),
            VMEM((sx + 6, n1, 9 * C), bf16),
            VMEM((sx + 4, n2, 9 * C), bf16),
            VMEM((sx + 2, ry, 9 * C), bf16),
            VMEM((sx + 4, n1, C), f32),
            VMEM((3, C, 9 * C), bf16),
            VMEM((9 * C, 2 * C), bf16),
            VMEM((sx + 2, n1, 3 * C), bf16),
            VMEM((sx + 2, n2, 3 * C), bf16),
            VMEM((D, 2, Q, width), bf16),
            VMEM((D, 2, Q, width), bf16),
            VMEM((D, Q, width), bf16),
            VMEM((D, Q, width), bf16),
            VMEM((D, Q, width), bf16),
            VMEM((D, Q, width), bf16),
            VMEM((D - 1, Q, width), bf16),
            VMEM((H, width), bf16),
            sem((D, 2, 2)), sem((D, 2, 2)), sem((D, 2)), sem((D, 2)), sem((D, 2)), sem((D, 2)),
            sem((D - 1, 2)), sem((D - 1, 2)), sem((3, 2)), sem((3, 2)), sem((2, 2)), sem((2, 2)),
        ],
        compiler_params=pltpu.CompilerParams(
            collective_id=0, has_side_effects=True, vmem_limit_bytes=50 * 2**20
        ),
        cost_estimate=pl.CostEstimate(flops=4 * 10**10, bytes_accessed=10**8, transcendentals=10**6),
        name="step",
    )(vol, cot, master, moment_one, moment_two)
    act, new_master, new_one, new_two = pl.pallas_call(
        finish_kernel,
        out_shape=(jax.ShapeDtypeStruct((sx, ry, width), bf16), table, table, table),
        in_specs=[whole] * 5,
        out_specs=(pl.BlockSpec(memory_space=HBM),) * 4,
        scratch_shapes=[VMEM((H, width), f32)] * 3 + [sem((13,))],
        compiler_params=pltpu.CompilerParams(vmem_limit_bytes=8 * 2**20),
        name="finish",
    )(act, rows, *held)
    return (act.reshape(volume.shape), new_master, new_one, new_two)


def solution(mesh):
    counts = (mesh.shape["dp"], mesh.shape["gx"], mesh.shape["gy"])
    return jax.shard_map(
        functools.partial(per_device, counts),
        mesh=mesh,
        in_specs=(
            P("dp", "gx", "gy", None, None),
            P("dp", "gx", "gy", None, None),
            P("dp", None),
            P("dp", None),
            P("dp", None),
        ),
        out_specs=(P("dp", "gx", "gy", None, None), P("dp", None), P("dp", None), P("dp", None)),
        check_vma=False,
    )
```

```python
import functools

import jax
import jax.numpy as jnp
from jax import lax
from jax.experimental import pallas as pl
from jax.experimental.pallas import tpu as pltpu
from jax.sharding import PartitionSpec as P

inv_root_two = 0.7071067811865476
inv_root_tau = 0.3989422804014327
beta_one = 0.9
beta_two = 0.999
learn_rate = 0.01
epsilon = 1e-08
C = 128
HX, HY, CY = 3, 4, 2
MESH = pl.DeviceIdType.MESH
VMEM, HBM = pltpu.VMEM, pltpu.HBM
f32, bf16 = jnp.float32, jnp.bfloat16


def gelu_value(field):
    return 0.5 * field * (1.0 + lax.erf(field * inv_root_two))


def gelu_slope(field):
    normal_cdf = 0.5 * (1.0 + lax.erf(field * inv_root_two))
    return normal_cdf + field * jnp.exp(-0.5 * field * field) * inv_root_tau


def place():
    d, x, y = lax.axis_index("dp"), lax.axis_index("gx"), lax.axis_index("gy")
    return d, x, y, lax.rem(x, 2), lax.rem(lax.div(y, 2), 2), lax.rem(y, 2)


def flip(index, bit, step):
    return index + step - 2 * step * bit


def gather_phases(counts, vol, cot, master_hbm, master, vext, cext, w, msem, hsend, hrecv, wsend, wrecv):
    D, GX, GY = counts
    d, x, y, bx, by, bc = place()
    sx, ry = vol.shape[0], vol.shape[1]
    H = master.shape[0]
    Q = H // 4
    N = 1
    part_rows = Q // N
    inner = (pl.ds(HX, sx), pl.ds(8 * HY, ry)), (pl.ds(1, sx), pl.ds(8 * CY, ry))
    load = pltpu.make_async_copy(master_hbm, master, msem.at[0])
    fields = [
        pltpu.make_async_copy(vol, vext.at[inner[0]], msem.at[1]),
        pltpu.make_async_copy(cot, cext.at[inner[1]], msem.at[2]),
    ]
    load.start()
    for copy in fields:
        copy.start()
    here = {"x": (d, flip(x, bx, 1), y), "y": (d, x, flip(y, by, 2)), "c": (d, x, flip(y, bc, 1))}

    for ref, hx, hy in ((vext, HX, 8 * HY), (cext, 1, 8 * CY)):
        end = jnp.zeros((hx, *ref.shape[1:]), bf16)
        side = jnp.zeros((sx, hy, C), bf16)
        ref[:hx] = end
        ref[hx + sx :] = end
        ref[hx : hx + sx, :hy] = side
        ref[hx : hx + sx, hy + ry :] = side
    around = [(i, j) for i in (-1, 0, 1) for j in (-1, 0, 1) if (i, j) != (0, 0)]

    def exists(i, j):
        ok = None
        for value, step, count in ((x, i, GX), (y, j, GY)):
            if step:
                now = (value + step >= 0) & (value + step < count)
                ok = now if ok is None else ok & now
        return ok

    barrier = pltpu.get_barrier_semaphore()
    total = jnp.int32(4)
    for target in (here["x"], here["y"], here["c"], (d, here["x"][1], here["y"][2])):
        pl.semaphore_signal(barrier, inc=1, device_id=target, device_id_type=MESH)
    for i, j in around:
        ok = exists(i, j)

        @pl.when(ok)
        def _(i=i, j=j):
            pl.semaphore_signal(barrier, inc=1, device_id=(d, x + i, y + j), device_id_type=MESH)

        total = total + jnp.where(ok, 1, 0)
    for t in range(1, D):
        pl.semaphore_signal(barrier, inc=1, device_id=(lax.rem(d + t, D), x, y), device_id_type=MESH)
    total = total + (D - 1)

    load.wait()
    w[pl.ds(pl.multiple_of(d * H, 16), H)] = master[...].astype(bf16)
    pl.semaphore_wait(barrier, total)

    def rows(s, q, n):
        return w.at[pl.ds(pl.multiple_of(s * H + q * Q + n * part_rows, 16), part_rows)]

    def move(ref, k, s, n, target):
        return pltpu.make_async_remote_copy(
            src_ref=ref, dst_ref=ref, send_sem=wsend.at[k, s, n], recv_sem=wrecv.at[k, s, n],
            device_id=target, device_id_type=MESH,
        )

    def bit(s):
        return jnp.where(lax.rem(s, 2) == 0, bx, by)

    def quarter(s):
        return 2 * bit(s) + bc

    def other(s):
        return 2 * (1 - bit(s)) + bc

    def up(s, n):
        return move(rows(s, quarter(s), n), 0, s, n, (d + 1, x, y))

    def down(s, n):
        return move(rows(s, quarter(s), n), 1, s, n, (d - 1, x, y))

    def partner(s, q, n):
        even = lax.rem(s, 2) == 0
        target = (d, jnp.where(even, here["x"][1], x), jnp.where(even, y, here["y"][2]))
        return move(rows(s, q, n), 2, s, n, target)

    def sibling(s, q, k, n):
        return move(rows(s, q, n), k, s, n, here["c"])

    @pl.when(d < D - 1)
    def _():
        for n in range(N):
            up(d, n).start()

    @pl.when(d > 0)
    def _():
        for n in range(N):
            down(d, n).start()

    def halo(n, i, j):
        def part(step, halo_x, size):
            if step < 0:
                return 0, halo_x + size, halo_x
            if step > 0:
                return size - halo_x, 0, halo_x
            return 0, halo_x, size

        copies = []
        for k, (src, dst, hx, hy) in enumerate(((vol, vext, HX, HY), (cot, cext, 1, CY))):
            xs, xd, xn = part(i, hx, sx)
            ys, yd, yn = part(j, 8 * hy, ry)
            copies.append(
                pltpu.make_async_remote_copy(
                    src_ref=src.at[pl.ds(xs, xn), pl.ds(ys, yn)],
                    dst_ref=dst.at[pl.ds(xd, xn), pl.ds(yd, yn)],
                    send_sem=hsend.at[k, n], recv_sem=hrecv.at[k, n],
                    device_id=(d, x + i, y + j), device_id_type=MESH,
                )
            )
        return copies

    for n, (i, j) in enumerate(around):
        @pl.when(exists(i, j))
        def _(n=n, i=i, j=j):
            for copy in halo(n, i, j):
                copy.start()

    def relay(t, n):
        for sign, line, more in ((-1, up, d < D - 1), (1, down, d > 0)):
            s = d + sign * t

            @pl.when((s >= 0) & (s < D))
            def _(s=s, line=line, more=more):
                line(s, n).wait_recv()

                @pl.when(more)
                def _():
                    line(s, n).start()

                partner(s, quarter(s), n).start()
                sibling(s, quarter(s), 3, n).start()

    def pass_on(t, n):
        for s in (d - t, d + t):
            @pl.when((s >= 0) & (s < D))
            def _(s=s):
                partner(s, other(s), n).wait_recv()
                sibling(s, other(s), 4, n).start()

    for n in range(N):
        relay(1, n)

    for n, (i, j) in enumerate(around):
        @pl.when(exists(i, j))
        def _(n=n, i=i, j=j):
            for copy in halo(7 - n, -i, -j):
                copy.wait_recv()

    for copy in fields:
        copy.wait()
    yield

    def settle(low, high):
        for s in range(low, high):
            @pl.when(d != s)
            def _(s=s):
                z = jnp.int32(s)
                for n in range(N):
                    sibling(z, 2 * bit(z) + 1 - bc, 3, n).wait_recv()
                    sibling(z, 2 * (1 - bit(z)) + 1 - bc, 4, n).wait_recv()

    for n in range(N):
        relay(2, n)
        pass_on(1, n)
        yield
    yield settle
    for t in range(3, D):
        for n in range(N):
            relay(t, n)
            pass_on(t - 1, n)
    for n in range(N):
        pass_on(D - 1, n)
    yield

    for s in range(D):
        z = jnp.int32(s)

        @pl.when(d != s)
        def _(z=z):
            for n in range(N):
                partner(z, quarter(z), n).wait_send()
                sibling(z, quarter(z), 3, n).wait_send()
                sibling(z, other(z), 4, n).wait_send()

        @pl.when((s <= d) & (d < D - 1))
        def _(z=z):
            for n in range(N):
                up(z, n).wait_send()

        @pl.when((s >= d) & (d > 0))
        def _(z=z):
            for n in range(N):
                down(z, n).wait_send()

    for n, (i, j) in enumerate(around):
        @pl.when(exists(i, j))
        def _(n=n, i=i, j=j):
            for copy in halo(n, i, j):
                copy.wait_send()

    yield


def shifted(field):
    rows = field.shape[0]
    z = lax.rem(lax.broadcasted_iota(jnp.int32, field.shape, 0), 8)
    before = jnp.where(z == 0, 0.0, pltpu.roll(field, 1, 0))
    after = jnp.where(z == 7, 0.0, pltpu.roll(field, rows - 1, 0))
    return before, field, after


def unfold(field, first, rows, out):
    views = shifted(field)
    for b in range(3):
        for c in range(3):
            k = 3 * b + c
            out[:, k * C : (k + 1) * C] = views[c][first + 8 * b : first + 8 * b + rows].astype(bf16)


def compute_phases(counts, vext, cext, w, act, grad, x1, x2, x3, first, kt, kk, d1, d2):
    D, GX, GY = counts
    sx = vext.shape[0] - 2 * HX
    ry = vext.shape[1] - 16 * HY
    gx, gy = lax.axis_index("gx"), lax.axis_index("gy")
    n1, n2 = ry + 32, ry + 16
    L = 9 * C

    d1[...] = jnp.zeros_like(d1)
    d2[...] = jnp.zeros_like(d2)

    cuts = 1
    edges = [(sx + 6) * k // cuts for k in range(cuts + 1)]
    for low, high in zip(edges, edges[1:]):
        @pl.loop(low, high)
        def _(s):
            unfold(vext[s].astype(f32), 8, n1, x1.at[s])

        yield

    def conv(source, pair, last, at, size, contract):
        def product(begin, slices, kernel):
            lhs = source[pl.ds(begin, slices)].reshape(slices * source.shape[1], L)
            return lax.dot_general(
                lhs, kernel, (((1,), (contract,)), ((), ())), preferred_element_type=f32
            )

        n = source.shape[1]
        both = product(at, size + 1, pair)
        return both[: size * n, :C] + both[n:, C:] + product(at + 2, size, last)

    def load_pair(base):
        for a in range(2):
            kk[:, a * C : (a + 1) * C] = w[base + a * L : base + (a + 1) * L]

    half = (sx + 4) // 2
    row = lax.broadcasted_iota(jnp.int32, (n1, C), 0)
    y_at = lax.div(row, 8) - 2 + gy * (ry // 8)
    y_ok = jnp.where((y_at >= 0) & (y_at < GY * (ry // 8)), 1.0, 0.0)

    def first_layer():
        load_pair(0)

        @pl.loop(0, 2)
        def _(p):
            pre = conv(x1, kk[...], w[2 * L : 3 * L], p * half, half, 0)
            for i in range(half):
                piece = pre[i * n1 : (i + 1) * n1]
                s = p * half + i
                first[s] = piece
                x_at = s - 2 + gx * sx
                x_ok = jnp.where((x_at >= 0) & (x_at < GX * sx), 1.0, 0.0)
                hidden = gelu_value(piece).astype(bf16).astype(f32) * (y_ok * x_ok)
                unfold(hidden, 0, n2, x2.at[s])

    yield first_layer

    for a in range(3):
        for k in range(9):
            base = (27 + 9 * (2 - a) + 8 - k) * C
            kt[a, :, k * C : (k + 1) * C] = w[base : base + C]

    half2 = (sx + 2) // 2
    load_pair(27 * C)

    @pl.loop(0, 2)
    def _(p):
        pre = conv(x2, kk[...], w[27 * C + 2 * L : 27 * C + 3 * L], p * half2, half2, 0)
        for i in range(half2):
            piece = pre[i * n2 : (i + 1) * n2]
            s = p * half2 + i
            up = cext[s].astype(f32)[8 : 8 + n2]
            delta = (up * gelu_slope(piece)).astype(bf16).astype(f32)
            unfold(delta, 0, ry, x3.at[s])

            @pl.when((s >= 1) & (s <= sx))
            def _():
                act[s - 1] = gelu_value(piece)[8 : 8 + ry].astype(bf16)
                r2 = lax.broadcasted_iota(jnp.int32, (n2, C), 0)
                inner = jnp.where((r2 >= 8) & (r2 < 8 + ry), delta, 0.0).astype(bf16)
                for a in range(3):
                    d2[s - 1 + a, :, a * C : (a + 1) * C] = inner

    def weight_grad(source, start, delta, base):
        n = delta.shape[1]
        rhs = delta[...].reshape((sx + 2) * n, 3 * C)

        @pl.loop(0, 3)
        def _(m):
            lanes = pl.ds(pl.multiple_of(m * 3 * C, C), 3 * C)
            lhs = source[pl.ds(start, sx + 2), :, lanes].reshape((sx + 2) * n, 3 * C)
            out = lax.dot_general(lhs, rhs, (((0,), (0,)), ((), ())), preferred_element_type=f32)
            for a in range(3):
                at = pl.multiple_of(base + a * L + m * 3 * C, C)
                grad[pl.ds(at, 3 * C)] = out[:, a * C : (a + 1) * C].astype(bf16)

    weight_grad(x2, 1, d2, 27 * C)
    yield

    back = conv(x3, kt[0:2].reshape(2 * C, L), kt[2], 0, sx, 1)
    for i in range(sx):
        piece = back[i * ry : (i + 1) * ry]
        slope = gelu_slope(first[i + 2][16 : 16 + ry])
        delta = (piece * slope).astype(bf16)
        for a in range(3):
            d1[i + a, 16 : 16 + ry, a * C : (a + 1) * C] = delta
    yield

    weight_grad(x1, 2, d1, 0)
    yield


def reduce_phases(counts, g, out, r1, a1, r2, a2, r3, a3, r4, fin, s1, q1, s2, q2, s3, q3, s4, q4, s5, q5, s6, q6):
    D, GX, GY = counts
    d, x, y, bx, by, bc = place()
    H = out.shape[0]
    Q = H // 4
    px, py, pc = (d, flip(x, bx, 1), y), (d, x, flip(y, by, 2)), (d, x, flip(y, bc, 1))
    pxy = (d, flip(x, bx, 1), flip(y, by, 2))
    chunks = ((0, Q),)
    NH = len(chunks)

    def copy(src, dst, send, recv, target):
        return pltpu.make_async_remote_copy(
            src_ref=src, dst_ref=dst, send_sem=send, recv_sem=recv, device_id=target, device_id_type=MESH
        )

    def in_quarter(s, q, lo, n):
        return pl.ds(pl.multiple_of(s * H + q * Q + lo, 16), n)

    def stage1(s, b, h):
        lo, n = chunks[h]
        src = g.at[in_quarter(s, 2 * b + 1 - bc, lo, n)]
        return copy(src, r1.at[s, b, pl.ds(lo, n)], s1.at[s, b, h], q1.at[s, b, h], pc)

    def bits(s):
        return (bx, by, px, py) if s % 2 == 0 else (by, bx, py, px)

    def stage2(s, h):
        b, _, target, _ = bits(s)
        at = pl.ds(*chunks[h])
        return copy(a1.at[s, 1 - b, at], r2.at[s, at], s2.at[s, h], q2.at[s, h], target)

    def halves(bit, h, body):
        lo, n = chunks[h]
        m = n // 32 * 16

        @pl.when(bit == 0)
        def _():
            body(lo, m, lo + m, n - m)

        @pl.when(bit == 1)
        def _():
            body(lo + m, n - m, lo, m)

    def stage3(s, h, lo, n):
        at = pl.ds(lo, n)
        return copy(a2.at[s, at], r3.at[s, at], s3.at[s, h], q3.at[s, h], bits(s)[3])

    def stage4(s, t, h, lo, n):
        at = pl.ds(lo, n)
        return copy(a3.at[s, at], r4.at[t - 1, at], s4.at[t - 1, h], q4.at[t - 1, h], (s, x, y))

    def stage6(b, c, h):
        lo, n = chunks[h]
        ref = fin.at[pl.ds(pl.multiple_of((2 * b + c) * Q + lo, 16), n)]
        return copy(ref, ref, s6.at[b, h], q6.at[b, h], pc)

    def begin(s, h):
        for b in range(2):
            stage1(s, b, h).start()

    def after1(s, h):
        lo, n = chunks[h]
        at = pl.ds(lo, n)
        for b in range(2):
            stage1(s, b, h).wait_recv()
            mine = g[in_quarter(s, 2 * b + bc, lo, n)].astype(f32)
            a1[s, b, at] = (mine + r1[s, b, at].astype(f32)).astype(bf16)
        stage2(s, h).start()

    def after2(s, h):
        at = pl.ds(*chunks[h])
        stage2(s, h).wait_recv()
        b = bits(s)[0]
        a2[s, at] = (a1[s, b, at].astype(f32) + r2[s, at].astype(f32)).astype(bf16)
        halves(bits(s)[1], h, lambda lo, n, olo, on: stage3(s, h, olo, on).start())

    def after3(s, h):
        def add(lo, n, olo, on):
            stage3(s, h, lo, n).wait_recv()
            at = pl.ds(lo, n)
            a3[s, at] = (a2[s, at].astype(f32) + r3[s, at].astype(f32)).astype(bf16)
            for t in range(1, D):
                @pl.when(lax.rem(d + t, D) == s)
                def _(t=t):
                    stage4(s, t, h, lo, n).start()

        halves(bits(s)[1], h, add)

    early, late = range(D // 2, D), range(D // 2)

    def each(group, *steps):
        for fn, h in steps:
            for s in group:
                fn(s, h)

    each(early, (begin, 0))
    yield
    each(early, (after1, 0))
    yield
    each(late, (begin, 0))
    yield
    each(early, (after2, 0))
    each(late, (after1, 0))
    each(early, (after3, 0))
    each(late, (after2, 0), (after3, 0))

    for s in range(D):
        for h in range(NH):
            for b in range(2):
                stage1(s, b, h).wait_send()
            stage2(s, h).wait_send()
            halves(bits(s)[1], h, lambda lo, n, olo, on, s=s, h=h: stage3(s, h, olo, on).wait_send())

    for s in range(D):
        @pl.when(d == s)
        def _(s=s):
            b, e, partner, across = bits(s)

            def piece(fb, lo, n):
                return fin.at[pl.ds(pl.multiple_of((2 * fb + bc) * Q + lo, 16), n)]

            def share(k, h, fb, lo, n, target):
                return copy(piece(fb, lo, n), piece(fb, lo, n), s5.at[k, h], q5.at[k, h], target)

            targets = (partner, across, pxy)

            def total(h, lo, n):
                at = pl.ds(lo, n)
                value = a3[s, at].astype(f32)
                for t in range(1, D):
                    stage4(s, t, h, lo, n).wait_recv()
                    value = value + r4[t - 1, at].astype(f32)
                piece(b, lo, n)[...] = value.astype(bf16)
                for k in range(3):
                    share(k, h, b, lo, n, targets[k]).start()

            def collect(h, lo, n, olo, on):
                share(0, h, 1 - b, lo, n, partner).wait_recv()
                share(1, h, b, olo, on, across).wait_recv()
                share(2, h, 1 - b, olo, on, pxy).wait_recv()

            for h in range(NH):
                halves(e, h, lambda lo, n, olo, on, h=h: total(h, lo, n))
            for h in range(NH):
                halves(e, h, lambda lo, n, olo, on, h=h: collect(h, lo, n, olo, on))
                for fb in range(2):
                    stage6(fb, bc, h).start()

    for s in range(D):
        for h in range(NH):
            def drain(lo, n, olo, on, s=s, h=h):
                for t in range(1, D):
                    @pl.when(lax.rem(d + t, D) == s)
                    def _(t=t):
                        stage4(s, t, h, lo, n).wait_send()

                @pl.when(d == s)
                def _():
                    for k in range(3):
                        ref = fin.at[pl.ds(lo, n)]
                        copy(ref, ref, s5.at[k, h], q5.at[k, h], pc).wait_send()

            halves(bits(s)[1], h, drain)

    for h in range(NH):
        for b in range(2):
            stage6(b, 1 - bc, h).wait_recv()
    out[...] = fin[...]

    for h in range(NH):
        for b in range(2):
            stage6(b, bc, h).wait_send()
    yield


def step_kernel(
    counts, vol, cot, master_hbm, one_hbm, two_hbm, act, out, master, one, two, vext, cext, w, g, *scratch
):
    msem, moves, fields, sums = scratch[0], scratch[1:5], scratch[5:13], scratch[13:]
    gather = gather_phases(counts, vol, cot, master_hbm, master, vext, cext, w, msem, *moves)
    compute = compute_phases(counts, vext, cext, w, act, g, *fields)
    reduce = reduce_phases(counts, g, out, *sums)
    next(gather)
    held = [
        pltpu.make_async_copy(one_hbm, one, msem.at[3]),
        pltpu.make_async_copy(two_hbm, two, msem.at[4]),
    ]
    for copy in held:
        copy.start()
    for _ in range(1):
        next(compute)
        next(gather)
    settle = next(gather)
    first_layer = next(compute)
    D = counts[0]
    low = lax.axis_index("dp") < D // 2

    @pl.when(low)
    def _():
        settle(0, D // 2)
        first_layer()

    next(gather)

    @pl.when(jnp.logical_not(low))
    def _():
        settle(0, D // 2)
        first_layer()

    settle(D // 2, D)
    next(compute)
    next(reduce)
    next(compute)
    next(reduce)
    next(compute)
    next(reduce)
    next(gather)
    next(reduce)
    for copy in held:
        copy.wait()


def finish_kernel(act_in, rows, master, one, two, act, new_master, new_one, new_two, o0, o1, o2, sem):
    H = master.shape[0]
    parts = 4
    n = H // parts
    copies = [pltpu.make_async_copy(act_in, act, sem.at[0])]
    copies[0].start()
    for i in range(parts):
        at = pl.ds(i * n, n)
        gradient = rows[at].astype(f32)
        first = beta_one * one[at] + (1.0 - beta_one) * gradient
        second = beta_two * two[at] + (1.0 - beta_two) * gradient * gradient
        o1[at] = first
        o2[at] = second
        step = first / (1.0 - beta_one**10) / (jnp.sqrt(second / (1.0 - beta_two**10)) + epsilon)
        o0[at] = master[at] - learn_rate * step
        for k, (src, dst) in enumerate(((o1, new_one), (o2, new_two), (o0, new_master))):
            copy = pltpu.make_async_copy(src.at[at], dst.at[at], sem.at[1 + 3 * i + k])
            copy.start()
            copies.append(copy)
    for copy in copies:
        copy.wait()


def per_device(counts, volume, cotangent, master, moment_one, moment_two):
    D, GX, GY = counts
    _, sx, sy, sz, width = volume.shape
    ry = sy * sz
    H = master.shape[0]
    Q = H // 4
    sem = pltpu.SemaphoreType.DMA
    whole = pl.BlockSpec(memory_space=VMEM)
    vol = volume.reshape(sx, ry, width)
    cot = cotangent.reshape(sx, ry, width)
    n1, n2 = ry + 32, ry + 16
    table = jax.ShapeDtypeStruct((H, width), f32)
    act, rows, *held = pl.pallas_call(
        functools.partial(step_kernel, counts),
        out_shape=(
            jax.ShapeDtypeStruct((sx, ry, width), bf16),
            jax.ShapeDtypeStruct((H, width), bf16),
            table,
            table,
            table,
        ),
        in_specs=[pl.BlockSpec(memory_space=HBM)] * 5,
        out_specs=(whole,) * 5,
        scratch_shapes=[
            VMEM((sx + 2 * HX, ry + 16 * HY, width), bf16),
            VMEM((sx + 2, ry + 16 * CY, width), bf16),
            VMEM((D * H, width), bf16),
            VMEM((D * H, width), bf16),
            sem((5,)), sem((2, 8)), sem((2, 8)), sem((5, D, 3)), sem((5, D, 3)),
            VMEM((sx + 6, n1, 9 * C), bf16),
            VMEM((sx + 4, n2, 9 * C), bf16),
            VMEM((sx + 2, ry, 9 * C), bf16),
            VMEM((sx + 4, n1, C), f32),
            VMEM((3, C, 9 * C), bf16),
            VMEM((9 * C, 2 * C), bf16),
            VMEM((sx + 2, n1, 3 * C), bf16),
            VMEM((sx + 2, n2, 3 * C), bf16),
            VMEM((D, 2, Q, width), bf16),
            VMEM((D, 2, Q, width), bf16),
            VMEM((D, Q, width), bf16),
            VMEM((D, Q, width), bf16),
            VMEM((D, Q, width), bf16),
            VMEM((D, Q, width), bf16),
            VMEM((D - 1, Q, width), bf16),
            VMEM((H, width), bf16),
            sem((D, 2, 2)), sem((D, 2, 2)), sem((D, 2)), sem((D, 2)), sem((D, 2)), sem((D, 2)),
            sem((D - 1, 2)), sem((D - 1, 2)), sem((3, 2)), sem((3, 2)), sem((2, 2)), sem((2, 2)),
        ],
        compiler_params=pltpu.CompilerParams(
            collective_id=0, has_side_effects=True, vmem_limit_bytes=50 * 2**20
        ),
        cost_estimate=pl.CostEstimate(flops=4 * 10**10, bytes_accessed=10**8, transcendentals=10**6),
        name="step",
    )(vol, cot, master, moment_one, moment_two)
    act, new_master, new_one, new_two = pl.pallas_call(
        finish_kernel,
        out_shape=(jax.ShapeDtypeStruct((sx, ry, width), bf16), table, table, table),
        in_specs=[whole] * 5,
        out_specs=(pl.BlockSpec(memory_space=HBM),) * 4,
        scratch_shapes=[VMEM((H, width), f32)] * 3 + [sem((13,))],
        compiler_params=pltpu.CompilerParams(vmem_limit_bytes=8 * 2**20),
        name="finish",
    )(act, rows, *held)
    return (act.reshape(volume.shape), new_master, new_one, new_two)


def solution(mesh):
    counts = (mesh.shape["dp"], mesh.shape["gx"], mesh.shape["gy"])
    return jax.shard_map(
        functools.partial(per_device, counts),
        mesh=mesh,
        in_specs=(
            P("dp", "gx", "gy", None, None),
            P("dp", "gx", "gy", None, None),
            P("dp", None),
            P("dp", None),
            P("dp", None),
        ),
        out_specs=(P("dp", "gx", "gy", None, None), P("dp", None), P("dp", None), P("dp", None)),
        check_vma=False,
    )
```
